32 devices in a mesh: dom: 4 (over z), bulk: 8 (over y, x, core).
Axes of the slice: x: 2, y: 2, z: 4, core: 2. Of those that a mesh axis runs over, the one named last changes fastest.
Arguments:
- node_patch: int32 [524288], P(('dom', 'bulk')), may hold values from 0 to 19999, as said below
- node_span: int32 [524288], P(('dom', 'bulk')), may hold values from 0 to 15
- start_grid: int32 [2, 524288], P(None, ('dom', 'bulk')), may hold values from 0 to 15
- target: float32 [3, 524288], P(None, ('dom', 'bulk')), may hold values from -0.1 to 1.1
- net: float32 [20000, 1024], P('bulk'), as said below
Outputs:
- placed: float32 [9, 524288], P(None, ('dom', 'bulk'))
The draws below stay inside these ranges and needn't reach their ends.
Inputs may be any that keep to these rules, and one draw needn't show every extreme that they name: In each partition's block of 16384 nodes (block k of the array, dom slowest), no owner node_patch // 2500 is named by more than 2560 nodes, and one owner is named by exactly 2560; that owner is the same for all blocks of one index of dom. `net`: component 3 (the weight) of every control point is positive.
All inputs are finite; a program needn't handle non-finite values.
Results may differ from the reference program's by a relative error of at most 0.0003.
Values sent between devices are 32-bit elements; how exact they have to be, the bound alone decides.
No kernel may reach another device: no remote copies, remote signals or barrier semaphores. Data moves between devices by JAX's collectives and lax.ppermute only.
A program may use at most 128 MiB of HBM per device.

```python
import jax
import jax.numpy as jnp
from jax import lax

NODE_DEV = 16384
PATCH_DEV = 2500
SPANS = 16
LEVELS = 16
ITERS = 4
CAP = 2560
OWNERS = 8
DOMS = 4
PATCHES = 20000
NODES = 524288


def draw_node_patch(key, part):
    blocks = NODES // NODE_DEV
    slots = OWNERS * CAP
    busy_key = jax.random.fold_in(key, 11)
    busy = jax.random.randint(busy_key, (DOMS,), 0, OWNERS)
    block_busy = jnp.repeat(busy, blocks // DOMS)

    def one_block(index, chosen):
        block_key = jax.random.fold_in(key, 1000 + index)
        ranks = jax.random.permutation(jax.random.fold_in(block_key, 1), slots)
        slot_owner = jnp.arange(slots) // CAP
        scores = ranks + (slot_owner != chosen).astype(jnp.int32) * slots
        order = jnp.argsort(scores, stable=True)[:NODE_DEV]
        owner = (order // CAP).astype(jnp.int32)
        owner = jax.random.permutation(jax.random.fold_in(block_key, 2), owner)
        local = jax.random.randint(jax.random.fold_in(block_key, 3), (NODE_DEV,), 0, PATCH_DEV)
        return (owner * PATCH_DEV + local).astype(jnp.int32)
    result = jax.vmap(one_block)(jnp.arange(blocks), block_busy)
    return result.reshape(NODES)


def draw_net(key, part):
    shape = (PATCHES, SPANS, 4, 4)
    first = jnp.arange(4, dtype=jnp.float32)[None, None, :, None] / 3.0
    second = jnp.arange(4, dtype=jnp.float32)[None, None, None, :] / 3.0
    rational_weight = jnp.exp(jax.random.uniform(jax.random.fold_in(key, 1), shape, jnp.float32, jnp.log(0.7), jnp.log(1.4)))
    coord_x = first + jax.random.uniform(jax.random.fold_in(key, 2), shape, jnp.float32, -0.1, 0.1)
    coord_y = second + jax.random.uniform(jax.random.fold_in(key, 3), shape, jnp.float32, -0.1, 0.1)
    height = jnp.clip(0.3 * jax.random.normal(jax.random.fold_in(key, 4), shape, jnp.float32), -1.0, 1.0)
    stacked = jnp.stack([rational_weight * coord_x, rational_weight * coord_y, rational_weight * height, rational_weight], axis=2)
    return stacked.reshape(PATCHES, 1024).astype(jnp.float32)


def plant(array, key, least, high):
    longest = array.shape.index(max(array.shape))
    spots = []
    for shift in (0, 1):
        where = [jax.random.randint(jax.random.fold_in(key, axis), (), 0, length) for axis, length in enumerate(array.shape)]
        where[longest] = (where[longest] + shift) % array.shape[longest]
        spots.append(tuple(where))
    return array.at[spots[0]].set(least).at[spots[1]].set(high)


def block_levels(own_key, dims, pieces, smallest, high):
    level, own = 1.0, jax.random.fold_in(own_key, 6)
    for dim, parts in pieces:
        steps = jnp.exp(jax.random.uniform(jax.random.fold_in(own, dim), (parts,), jnp.float32, smallest / len(pieces), high / len(pieces)))
        level = level * jnp.repeat(steps, dims[dim] // parts).reshape([-1 if axis == dim else 1 for axis in range(len(dims))])
    return level


def setup_inputs(seed: int = 0) -> dict:
    keys = jax.random.split(jax.random.key(seed), 6)
    return {
        "node_patch": draw_node_patch(jax.random.fold_in(keys[5], 71), 0),
        "node_span": plant(jax.random.randint(keys[1], (NODES,), 0, SPANS), jax.random.fold_in(keys[1], 1), 0, SPANS - 1).astype(jnp.int32),
        "start_grid": plant(jax.random.randint(keys[2], (2, NODES), 0, LEVELS), jax.random.fold_in(keys[2], 1), 0, LEVELS - 1).astype(jnp.int32),
        "target": jnp.clip(-0.1 + 1.2 * jax.random.uniform(keys[3], (3, NODES), jnp.float32) ** block_levels(keys[3], (3, NODES), ((1, 32),), -0.2, 0.2), -0.1, 1.1),
        "net": draw_net(jax.random.fold_in(keys[5], 71), 0),
    }


damping = 0.1


def bernstein(param):
    other = 1.0 - param
    value = jnp.stack([other * other * other, 3.0 * param * other * other, 3.0 * param * param * other, param * param * param])
    slope = jnp.stack([-3.0 * other * other, 3.0 * other * other - 6.0 * param * other, 6.0 * param * other - 3.0 * param * param, 3.0 * param * param])
    return value, slope


def surface(control, upar, vpar):
    base_u, slope_u = bernstein(upar)
    basis_along_vdir, slope_vdir = bernstein(vpar)
    mixed_partial = jnp.sum(base_u[None, :, None, :] * control, axis=1)
    mixed_partial_udir = jnp.sum(slope_u[None, :, None, :] * control, axis=1)
    homogeneous_point = jnp.sum(basis_along_vdir[None] * mixed_partial, axis=1)
    homogeneous_udiff = jnp.sum(basis_along_vdir[None] * mixed_partial_udir, axis=1)
    homogeneous_vdiff = jnp.sum(slope_vdir[None] * mixed_partial, axis=1)
    rational_weight = homogeneous_point[3]
    surface_point = homogeneous_point[:3] / rational_weight
    tangent_udir = (homogeneous_udiff[:3] - surface_point * homogeneous_udiff[3]) / rational_weight
    tangent_vdir = (homogeneous_vdiff[:3] - surface_point * homogeneous_vdiff[3]) / rational_weight
    return surface_point, tangent_udir, tangent_vdir


def project(coeffs, goal, start):
    control = coeffs.reshape(4, 4, 4, -1)
    upar = start[0]
    vpar = start[1]
    for step in range(ITERS):
        surface_point, tangent_udir, tangent_vdir = surface(control, upar, vpar)
        miss = surface_point - goal
        grad_u = jnp.sum(tangent_udir * miss, axis=0)
        grad_v = jnp.sum(tangent_vdir * miss, axis=0)
        h_uu = jnp.sum(tangent_udir * tangent_udir, axis=0) + damping
        h_vv = jnp.sum(tangent_vdir * tangent_vdir, axis=0) + damping
        h_uv = jnp.sum(tangent_udir * tangent_vdir, axis=0)
        determ = h_uu * h_vv - h_uv * h_uv
        upar = jnp.clip(upar - (h_vv * grad_u - h_uv * grad_v) / determ, 0.0, 1.0)
        vpar = jnp.clip(vpar - (h_uu * grad_v - h_uv * grad_u) / determ, 0.0, 1.0)
    surface_point, tangent_udir, tangent_vdir = surface(control, upar, vpar)
    return jnp.concatenate([surface_point, tangent_udir, tangent_vdir], axis=0)


def reference(node_patch, node_span, start_grid, target, net):
    all_rows = net.reshape(-1, 64)
    row_index = (node_patch * SPANS + node_span).astype(jnp.int32)
    blocks = NODES // NODE_DEV

    def one_block(packed):
        rows, levels, goal = packed
        coeffs = all_rows[rows].T
        start = (levels.astype(jnp.float32) + 0.5) / LEVELS
        return project(coeffs, goal, start)

    result = lax.map(one_block, (row_index.reshape(blocks, NODE_DEV),
                                 start_grid.reshape(2, blocks, NODE_DEV).transpose(1, 0, 2),
                                 target.reshape(3, blocks, NODE_DEV).transpose(1, 0, 2)))
    return result.transpose(1, 0, 2).reshape(9, NODES)
```

```python
import functools

import jax
import jax.numpy as jnp
from jax import lax
from jax.experimental import pallas as pl
from jax.experimental.pallas import tpu as pltpu
from jax.sharding import PartitionSpec as P

SPANS = 16
LEVELS = 16
ITERS = 4
LANES = 128
SENT = 6
GIVEN = 9

damping = 0.1


def round_up(value, unit):
    return -(-value // unit) * unit


def iota(shape, dim):
    return lax.broadcasted_iota(jnp.int32, shape, dim)


def route_kernel(owners, windows, patch_dev, patch_pad, patch_ref, span_ref, grid_ref, target_ref,
                 sent_ref, key_ref, first_ref, code_ref, load_ref, slot_ref, first_smem, sem):
    blocks = patch_ref.shape[0]
    patch = patch_ref[...]
    owner = jnp.zeros_like(patch)
    for o in range(1, owners):
        owner += (patch >= o * patch_dev).astype(jnp.int32)
    span = span_ref[...]
    row = 2 * ((span >> 1) * patch_pad + patch - owner * patch_dev) + (span & 1)

    lane = iota((LANES, LANES), 1)
    sub = iota((LANES, LANES), 0)
    upto = (sub <= lane).astype(jnp.bfloat16)
    every = jnp.ones((LANES, LANES), jnp.bfloat16)
    counter = jnp.concatenate([upto, every], axis=1)
    earlier = (iota((blocks, blocks), 1) < iota((blocks, blocks), 0)).astype(jnp.bfloat16)
    blane = iota((blocks, LANES), 1)
    diagonal = iota((blocks, blocks), 0) == iota((blocks, blocks), 1)

    within = jnp.zeros_like(patch)
    for o in range(owners):
        mine = owner == o
        mask = mine.astype(jnp.bfloat16)
        counts = jnp.dot(mask, counter, preferred_element_type=jnp.float32)
        total = counts[:, LANES:]
        offset = jnp.dot(earlier, total.astype(jnp.bfloat16), preferred_element_type=jnp.float32).astype(jnp.int32)
        before = counts[:, :LANES].astype(jnp.int32) - mine.astype(jnp.int32)
        total = total.astype(jnp.int32)
        within = jnp.where(mine, before + offset, within)
        first = jnp.sum(jnp.where(diagonal, offset.astype(jnp.float32), 0.0), axis=0, keepdims=True)
        first_ref[o:o + 1, :] = first.astype(jnp.int32) >> 7
        word = jnp.where(mine, blane + LANES * (blane - before), 0)
        for bit in range(7):
            moves = 1 << (7 + bit)
            coming = pltpu.roll(word, LANES - (1 << bit), 1)
            word = jnp.where((coming & moves) != 0, coming, jnp.where((word & moves) != 0, 0, word))
        edge = offset & (LANES - 1)
        rank = (blane - edge) & (LANES - 1)
        source = jnp.take_along_axis(word & (LANES - 1), rank, axis=1)
        valid = rank < total
        code = source + jnp.where(valid, jnp.where(blane >= edge, 128, 256), 0)
        code_ref[o * blocks:(o + 1) * blocks, :] = code

    key_ref[...] = (owner * (windows + 1) * LANES) + within
    copy = pltpu.make_async_copy(first_ref, first_smem, sem)
    copy.start()

    slot_ref[...] = jnp.zeros_like(slot_ref)
    rowf = row.astype(jnp.float32)
    load_ref[...] = jnp.zeros_like(load_ref)
    for b in range(blocks):
        load_ref[8 * b:8 * b + 3, :] = target_ref[:, b * LANES:(b + 1) * LANES]
        load_ref[8 * b + 3:8 * b + 5, :] = (grid_ref[:, b * LANES:(b + 1) * LANES].astype(jnp.float32) + 0.5) * (1.0 / LEVELS)
        load_ref[8 * b + 5:8 * b + 6, :] = rowf[b:b + 1, :]
    copy.wait()

    def place(b, carry):
        load = load_ref[pl.ds(pl.multiple_of(8 * b, 8), 8), :]
        for o in range(owners):
            code = jnp.broadcast_to(code_ref[pl.ds(o * blocks + b, 1), :], (8, LANES))
            moved = jnp.take_along_axis(load, code & (LANES - 1), axis=1)
            base = pl.multiple_of((o * (windows + 1) + first_smem[o, b]) * 8, 8)
            pltpu.store(slot_ref.at[pl.ds(base, 8), :], moved, mask=(code & 128) != 0)
            pltpu.store(slot_ref.at[pl.ds(base + 8, 8), :], moved, mask=(code & 256) != 0)
        return carry

    lax.fori_loop(0, blocks, place, 0)

    for o in range(owners):
        for c in range(SENT):
            for w in range(0, windows, 8):
                size = min(8, windows - w)
                rows = slot_ref[pl.ds((o * (windows + 1) + w) * 8 + c, size, stride=8), :]
                sent_ref[o, c * windows + w:c * windows + w + size, :] = rows


def route(node_patch, node_span, start_grid, target, owners, windows, patch_dev, patch_pad):
    nodes = node_patch.shape[0]
    blocks = nodes // LANES
    return pl.pallas_call(
        functools.partial(route_kernel, owners, windows, patch_dev, patch_pad),
        out_shape=(
            jax.ShapeDtypeStruct((owners, SENT * windows, LANES), jnp.float32),
            jax.ShapeDtypeStruct((blocks, LANES), jnp.int32),
            jax.ShapeDtypeStruct((owners, blocks), jnp.int32),
        ),
        in_specs=[pl.BlockSpec(memory_space=pltpu.VMEM)] * 4,
        out_specs=[pl.BlockSpec(memory_space=pltpu.VMEM)] * 3,
        scratch_shapes=[
            pltpu.VMEM((owners * blocks, LANES), jnp.int32),
            pltpu.VMEM((8 * blocks, LANES), jnp.float32),
            pltpu.VMEM((owners * (windows + 1) * 8, LANES), jnp.float32),
            pltpu.SMEM((owners, blocks), jnp.int32),
            pltpu.SemaphoreType.DMA,
        ],
        compiler_params=pltpu.CompilerParams(vmem_limit_bytes=40 * 2**20),
        name="route",
    )(node_patch.reshape(blocks, LANES), node_span.reshape(blocks, LANES), start_grid, target)


def bernstein(param):
    other = 1.0 - param
    square, cross, low = other * other, param * other, param * param
    value = (other * square, 3.0 * cross * other, 3.0 * param * cross, param * low)
    slope = (-3.0 * square, 3.0 * square - 6.0 * cross, 6.0 * cross - 3.0 * low, 3.0 * low)
    return value, slope


def weighted(weights, values):
    return (weights[0] * values[0] + weights[1] * values[1]) + (weights[2] * values[2] + weights[3] * values[3])


def surface(read, upar, vpar):
    base_u, slope_u = bernstein(upar)
    base_v, slope_v = bernstein(vpar)
    point, along_u, along_v = [], [], []
    for c in range(4):
        mixed, mixed_u = [], []
        for j in range(4):
            column = [read(c * 16 + i * 4 + j) for i in range(4)]
            mixed.append(weighted(base_u, column))
            mixed_u.append(weighted(slope_u, column))
        point.append(weighted(base_v, mixed))
        along_u.append(weighted(base_v, mixed_u))
        along_v.append(weighted(slope_v, mixed))
    inverse = 1.0 / point[3]
    position = [point[c] * inverse for c in range(3)]
    tangent_u = [(along_u[c] - position[c] * along_u[3]) * inverse for c in range(3)]
    tangent_v = [(along_v[c] - position[c] * along_v[3]) * inverse for c in range(3)]
    return position, tangent_u, tangent_v


def inner(left, right):
    return left[0] * right[0] + left[1] * right[1] + left[2] * right[2]


def project(read, goal, upar, vpar):
    for _ in range(ITERS):
        position, tangent_u, tangent_v = surface(read, upar, vpar)
        miss = [position[c] - goal[c] for c in range(3)]
        grad_u = inner(tangent_u, miss)
        grad_v = inner(tangent_v, miss)
        h_uu = inner(tangent_u, tangent_u) + damping
        h_vv = inner(tangent_v, tangent_v) + damping
        h_uv = inner(tangent_u, tangent_v)
        inverse = 1.0 / (h_uu * h_vv - h_uv * h_uv)
        upar = jnp.clip(upar - (h_vv * grad_u - h_uv * grad_v) * inverse, 0.0, 1.0)
        vpar = jnp.clip(vpar - (h_uu * grad_v - h_uv * grad_u) * inverse, 0.0, 1.0)
    position, tangent_u, tangent_v = surface(read, upar, vpar)
    return position + tangent_u + tangent_v


def project_kernel(sources, windows, given_pad, got_ref, net_ref, out_ref,
                   net_vmem, index_ref, index_smem, tile_ref, coeff_ref, net_sem, index_sem):
    patches = net_ref.shape[0]
    chunks = net_ref.shape[1] // LANES
    patch_pad = net_vmem.shape[0] // chunks
    groups = sources // 8
    sent = SENT * windows
    loads = []
    for c in range(chunks):
        loads.append(pltpu.make_async_copy(
            net_ref.at[:, pl.ds(c * LANES, LANES)], net_vmem.at[pl.ds(c * patch_pad, patches), :], net_sem.at[c]))
        loads[-1].start()

    def arrived(g, c, w):
        return got_ref[pl.ds(g * 8 * sent + c * windows + w, 8, stride=sent), :]

    for w in range(windows):
        for g in range(groups):
            code = arrived(g, 5, w).astype(jnp.int32)
            index_ref[pl.ds((w * groups + g) * 8, 8), :] = code >> 1
    copy = pltpu.make_async_copy(index_ref, index_smem, index_sem)
    copy.start()
    copy.wait()
    for load in loads:
        load.wait()

    def group_step(t, carry):
        w = t // groups
        g = t - w * groups
        code = arrived(g, 5, w).astype(jnp.int32)
        odd = (code & 1) == 1
        for s in range(8):
            for i in range(LANES):
                at = index_smem[t * 8 + s, i]
                tile_ref[s * LANES + i:s * LANES + i + 1, :] = net_vmem[pl.ds(at, 1), :]
            both = tile_ref[s * LANES:(s + 1) * LANES, :].T
            picked = jnp.where(odd[s:s + 1, :], both[64:, :], both[:64, :])
            coeff_ref[pl.ds(s, 64, stride=8), :] = picked

        def read(k):
            return coeff_ref[8 * k:8 * k + 8, :]

        goal = [arrived(g, c, w) for c in range(3)]
        result = project(read, goal, arrived(g, 3, w), arrived(g, 4, w))
        for c in range(GIVEN):
            out_ref[pl.ds(g * 8 * given_pad + c * windows + w, 8, stride=given_pad), :] = result[c]
        return carry

    lax.fori_loop(0, windows * groups, group_step, 0)


def project_nodes(got, net, windows, patch_pad, given_pad):
    sources = got.shape[0]
    chunks = net.shape[1] // LANES
    tiles = windows * sources
    return pl.pallas_call(
        functools.partial(project_kernel, sources, windows, given_pad),
        out_shape=jax.ShapeDtypeStruct((sources * given_pad, LANES), jnp.float32),
        in_specs=[pl.BlockSpec(memory_space=pltpu.VMEM), pl.BlockSpec(memory_space=pl.ANY)],
        out_specs=pl.BlockSpec(memory_space=pltpu.VMEM),
        scratch_shapes=[
            pltpu.VMEM((chunks * patch_pad, LANES), jnp.float32),
            pltpu.VMEM((tiles, LANES), jnp.int32),
            pltpu.SMEM((tiles, LANES), jnp.int32),
            pltpu.VMEM((8 * LANES, LANES), jnp.float32),
            pltpu.VMEM((64 * 8, LANES), jnp.float32),
            pltpu.SemaphoreType.DMA((chunks,)),
            pltpu.SemaphoreType.DMA,
        ],
        compiler_params=pltpu.CompilerParams(vmem_limit_bytes=40 * 2**20),
        name="project",
    )(got.reshape(sources * SENT * windows, LANES), net)


def return_kernel(owners, windows, given_pad, key_ref, first_smem, got_ref, out_ref):
    blocks = key_ref.shape[0]
    sub = iota((8, LANES), 0)

    def fetch(b, carry):
        key = jnp.broadcast_to(key_ref[pl.ds(b, 1), :], (8, LANES))
        lane = key & (LANES - 1)
        key = key >> 7
        rest = key - sub
        main = jnp.zeros((8, LANES), jnp.float32)
        last = jnp.zeros((8, LANES), jnp.float32)
        for o in range(owners):
            w = first_smem[o, b]
            for step in range(2):
                at = jnp.minimum(w + step, windows - 1)
                rows = got_ref[pl.ds(o * given_pad + at, 8, stride=windows), :]
                moved = jnp.take_along_axis(rows, lane, axis=1)
                main = jnp.where(key == o * (windows + 1) + at, moved, main)
            at = jnp.minimum(w, windows - 8)
            rows = got_ref[pl.ds(o * given_pad + 8 * windows + at, 8), :]
            moved = jnp.take_along_axis(rows, lane, axis=1)
            last = jnp.where(rest == o * (windows + 1) + at, moved, last)
        at = pl.ds(pl.multiple_of(b * LANES, LANES), LANES)
        out_ref[0:8, at] = main
        out_ref[8:9, at] = jnp.sum(last, axis=0, keepdims=True)
        return carry

    lax.fori_loop(0, blocks, fetch, 0)


def return_nodes(key, first, got, windows, given_pad):
    owners, blocks = first.shape
    return pl.pallas_call(
        functools.partial(return_kernel, owners, windows, given_pad),
        out_shape=jax.ShapeDtypeStruct((GIVEN, blocks * LANES), jnp.float32),
        in_specs=[
            pl.BlockSpec(memory_space=pltpu.VMEM),
            pl.BlockSpec(memory_space=pltpu.SMEM),
            pl.BlockSpec(memory_space=pltpu.VMEM),
        ],
        out_specs=pl.BlockSpec(memory_space=pltpu.VMEM),
        compiler_params=pltpu.CompilerParams(vmem_limit_bytes=40 * 2**20),
        name="give_back",
    )(key, first, got.reshape(owners * given_pad, LANES))


def body(node_patch, node_span, start_grid, target, net):
    owners = lax.axis_size("bulk")
    patch_dev = net.shape[0]
    patch_pad = round_up(patch_dev, 8)
    nodes = node_patch.shape[0]
    windows = nodes * 5 // 32 // LANES
    given_pad = round_up(GIVEN * windows, 8)
    sent, key, first = route(node_patch, node_span, start_grid, target, owners, windows, patch_dev, patch_pad)
    got = lax.all_to_all(sent, "bulk", split_axis=0, concat_axis=0, tiled=True)
    placed = project_nodes(got, net, windows, patch_pad, given_pad)
    answered = lax.all_to_all(
        placed.reshape(owners, given_pad, LANES), "bulk", split_axis=0, concat_axis=0, tiled=True)
    return return_nodes(key, first, answered, windows, given_pad)


def solution(mesh):
    return jax.shard_map(
        body,
        mesh=mesh,
        in_specs=(
            P(("dom", "bulk")),
            P(("dom", "bulk")),
            P(None, ("dom", "bulk")),
            P(None, ("dom", "bulk")),
            P("bulk", None),
        ),
        out_specs=P(None, ("dom", "bulk")),
        check_vma=False,
    )
```

```python
import functools

import jax
import jax.numpy as jnp
from jax import lax
from jax.experimental import pallas as pl
from jax.experimental.pallas import tpu as pltpu
from jax.sharding import PartitionSpec as P

SPANS = 16
LEVELS = 16
ITERS = 4
LANES = 128
SENT = 6
GIVEN = 9
UNROLL = 8

damping = 0.1


def round_up(value, unit):
    return -(-value // unit) * unit


def iota(shape, dim):
    return lax.broadcasted_iota(jnp.int32, shape, dim)


def take_lanes(rows, lane):
    return jnp.take_along_axis(rows, lane, axis=1, mode="promise_in_bounds")


def route_kernel(owners, windows, patch_dev, patch_hbm, span_hbm, grid_hbm, target_hbm, net_hbm,
                 sent_ref, key_ref, first_ref, net_ref,
                 patch_ref, span_ref, grid_ref, target_ref,
                 code_ref, load_ref, slot_ref, first_smem, in_sem, net_sem, first_sem):
    copies = []
    for k, (source, to) in enumerate(
            ((patch_hbm, patch_ref), (span_hbm, span_ref), (grid_hbm, grid_ref), (target_hbm, target_ref))):
        copies.append(pltpu.make_async_copy(source, to, in_sem.at[k]))
        copies[-1].start()
    chunks = net_hbm.shape[1] // LANES
    patch_pad = net_ref.shape[0] // chunks
    loads = []
    for c in range(chunks):
        loads.append(pltpu.make_async_copy(
            net_hbm.at[:, pl.ds(c * LANES, LANES)], net_ref.at[pl.ds(c * patch_pad, patch_dev), :], net_sem.at[c]))
        loads[-1].start()
    slot_ref[...] = jnp.zeros_like(slot_ref)
    blocks = patch_ref.shape[0]
    copies[0].wait()
    patch = patch_ref[...]
    owner = jnp.zeros_like(patch)
    for o in range(1, owners):
        owner += (patch >= o * patch_dev).astype(jnp.int32)

    lane = iota((LANES, LANES), 1)
    sub = iota((LANES, LANES), 0)
    upto = (sub <= lane).astype(jnp.bfloat16)
    every = jnp.ones((LANES, LANES), jnp.bfloat16)
    counter = jnp.concatenate([upto, every], axis=1)
    earlier = (iota((blocks, blocks), 1) < iota((blocks, blocks), 0)).astype(jnp.bfloat16)
    blane = iota((blocks, LANES), 1)
    diagonal = iota((blocks, blocks), 0) == iota((blocks, blocks), 1)

    key = jnp.zeros_like(patch)
    for o in range(owners):
        mine = owner == o
        mask = mine.astype(jnp.bfloat16)
        counts = jnp.dot(mask, counter, preferred_element_type=jnp.float32)
        total = counts[:, LANES:]
        offset = jnp.dot(earlier, total.astype(jnp.bfloat16), preferred_element_type=jnp.float32).astype(jnp.int32)
        before = counts[:, :LANES].astype(jnp.int32) - mine.astype(jnp.int32)
        total = total.astype(jnp.int32)
        edge = offset & (LANES - 1)
        key = jnp.where(mine, before + edge + 2 * LANES * o, key)
        first = jnp.sum(jnp.where(diagonal, offset.astype(jnp.float32), 0.0), axis=0, keepdims=True)
        first_ref[o:o + 1, :] = first.astype(jnp.int32) >> 7
        word = jnp.where(mine, blane + LANES * (blane - before), 0)
        for bit in range(7):
            moves = 1 << (7 + bit)
            coming = pltpu.roll(word, LANES - (1 << bit), 1)
            word = jnp.where((coming & moves) != 0, coming, jnp.where((word & moves) != 0, 0, word))
        rank = (blane - edge) & (LANES - 1)
        source = take_lanes(word & (LANES - 1), rank)
        valid = rank < total
        code_ref[o * blocks:(o + 1) * blocks, :] = source + jnp.where(valid, jnp.where(blane >= edge, 128, 256), 0)

    key_ref[...] = key
    copy = pltpu.make_async_copy(first_ref, first_smem, first_sem)
    copy.start()
    for waiting in copies[1:]:
        waiting.wait()
    span = span_ref[...]
    row = (2 * ((span >> 1) * patch_pad + patch - owner * patch_dev) + (span & 1)).astype(jnp.float32)
    for b in range(blocks):
        load_ref[8 * b:8 * b + 3, :] = target_ref[:, b * LANES:(b + 1) * LANES]
        load_ref[8 * b + 3:8 * b + 5, :] = (grid_ref[:, b * LANES:(b + 1) * LANES].astype(jnp.float32) + 0.5) * (1.0 / LEVELS)
        load_ref[8 * b + 5:8 * b + 6, :] = row[b:b + 1, :]
    copy.wait()

    def place(step, carry):
        for k in range(UNROLL):
            b = step * UNROLL + k
            load = load_ref[pl.ds(pl.multiple_of(8 * b, 8), 8), :]
            for o in range(owners):
                code = jnp.broadcast_to(code_ref[pl.ds(o * blocks + b, 1), :], (8, LANES))
                moved = take_lanes(load, code & (LANES - 1))
                base = pl.multiple_of((o * (windows + 1) + first_smem[o, b]) * 8, 8)
                pltpu.store(slot_ref.at[pl.ds(base, 8), :], moved, mask=(code & 128) != 0)
                pltpu.store(slot_ref.at[pl.ds(base + 8, 8), :], moved, mask=(code & 256) != 0)
        return carry

    lax.fori_loop(0, blocks // UNROLL, place, 0)

    for o in range(owners):
        for c in range(SENT):
            for w in range(0, windows, 8):
                size = min(8, windows - w)
                rows = slot_ref[pl.ds((o * (windows + 1) + w) * 8 + c, size, stride=8), :]
                sent_ref[o, c * windows + w:c * windows + w + size, :] = rows
    for waiting in loads:
        waiting.wait()


def route(node_patch, node_span, start_grid, target, net, owners, windows):
    nodes = node_patch.shape[0]
    blocks = nodes // LANES
    patch_dev = net.shape[0]
    chunks = net.shape[1] // LANES
    patch_pad = round_up(patch_dev, 8)
    return pl.pallas_call(
        functools.partial(route_kernel, owners, windows, patch_dev),
        out_shape=(
            jax.ShapeDtypeStruct((owners, SENT * windows, LANES), jnp.float32),
            jax.ShapeDtypeStruct((blocks, LANES), jnp.int32),
            jax.ShapeDtypeStruct((owners, blocks), jnp.int32),
            jax.ShapeDtypeStruct((chunks * patch_pad, LANES), jnp.float32),
        ),
        in_specs=[pl.BlockSpec(memory_space=pltpu.HBM)] * 5,
        out_specs=[pl.BlockSpec(memory_space=pltpu.VMEM)] * 4,
        scratch_shapes=[
            pltpu.VMEM((blocks, LANES), jnp.int32),
            pltpu.VMEM((blocks, LANES), jnp.int32),
            pltpu.VMEM(start_grid.shape, jnp.int32),
            pltpu.VMEM(target.shape, jnp.float32),
            pltpu.VMEM((owners * blocks, LANES), jnp.int32),
            pltpu.VMEM((8 * blocks, LANES), jnp.float32),
            pltpu.VMEM((owners * (windows + 1) * 8, LANES), jnp.float32),
            pltpu.SMEM((owners, blocks), jnp.int32),
            pltpu.SemaphoreType.DMA((4,)),
            pltpu.SemaphoreType.DMA((chunks,)),
            pltpu.SemaphoreType.DMA,
        ],
        compiler_params=pltpu.CompilerParams(vmem_limit_bytes=40 * 2**20),
        name="route",
    )(node_patch.reshape(blocks, LANES), node_span.reshape(blocks, LANES), start_grid, target, net)


def bernstein(param):
    other = 1.0 - param
    square, cross, low = other * other, param * other, param * param
    value = (other * square, 3.0 * cross * other, 3.0 * param * cross, param * low)
    slope = (-3.0 * square, 3.0 * square - 6.0 * cross, 6.0 * cross - 3.0 * low, 3.0 * low)
    return value, slope


def weighted(weights, values):
    return (weights[0] * values[0] + weights[1] * values[1]) + (weights[2] * values[2] + weights[3] * values[3])


def surface(read, upar, vpar, answer):
    base_u, slope_u = bernstein(upar)
    base_v, slope_v = bernstein(vpar)
    yield
    point, along_u, along_v = [], [], []
    for c in range(4):
        mixed, mixed_u = [], []
        for j in range(4):
            column = [read(c * 16 + i * 4 + j) for i in range(4)]
            mixed.append(weighted(base_u, column))
            mixed_u.append(weighted(slope_u, column))
            yield
        point.append(weighted(base_v, mixed))
        along_u.append(weighted(base_v, mixed_u))
        along_v.append(weighted(slope_v, mixed))
        yield
    inverse = 1.0 / point[3]
    position = [point[c] * inverse for c in range(3)]
    yield
    tangent_u = [(along_u[c] - position[c] * along_u[3]) * inverse for c in range(3)]
    tangent_v = [(along_v[c] - position[c] * along_v[3]) * inverse for c in range(3)]
    yield
    answer.extend((position, tangent_u, tangent_v))


def inner(left, right):
    return left[0] * right[0] + left[1] * right[1] + left[2] * right[2]


def project(read, goal, start, finish):
    upar, vpar = start()
    goal = goal()
    for _ in range(ITERS):
        answer = []
        yield from surface(read, upar, vpar, answer)
        position, tangent_u, tangent_v = answer
        miss = [position[c] - goal[c] for c in range(3)]
        grad_u = inner(tangent_u, miss)
        grad_v = inner(tangent_v, miss)
        yield
        h_uu = inner(tangent_u, tangent_u) + damping
        h_vv = inner(tangent_v, tangent_v) + damping
        h_uv = inner(tangent_u, tangent_v)
        yield
        inverse = 1.0 / (h_uu * h_vv - h_uv * h_uv)
        upar = jnp.clip(upar - (h_vv * grad_u - h_uv * grad_v) * inverse, 0.0, 1.0)
        vpar = jnp.clip(vpar - (h_uu * grad_v - h_uv * grad_u) * inverse, 0.0, 1.0)
        yield
    answer = []
    yield from surface(read, upar, vpar, answer)
    finish(answer[0] + answer[1] + answer[2])


PROJECT_STEPS = ITERS * 27 + 25


def project_kernel(sources, windows, given_pad, got_ref, net_ref, out_ref,
                   index_ref, index_even, index_odd, tile_ref, coeff_even, coeff_odd, index_sem):
    groups = sources // 8
    sent = SENT * windows
    total = windows * groups
    indices, coeffs = (index_even, index_odd), (coeff_even, coeff_odd)

    def arrived(t, c):
        w, g = t // groups, t % groups
        return got_ref[pl.ds(g * 8 * sent + c * windows + w, 8, stride=sent), :]

    def fetch(t, parity):
        return pltpu.make_async_copy(
            index_ref.at[pl.ds(pl.multiple_of(8 * t, 8), 8), :], indices[parity], index_sem.at[parity])

    def gather(t, parity):
        index, coeff = indices[parity], coeffs[parity]
        odd = (arrived(t, 5).astype(jnp.int32) & 1) == 1
        for s in range(8):
            for i in range(LANES):
                tile_ref[s * LANES + i:s * LANES + i + 1, :] = net_ref[pl.ds(index[s, i], 1), :]
                yield
            both = tile_ref[s * LANES:(s + 1) * LANES, :].T
            coeff[pl.ds(s, 64, stride=8), :] = jnp.where(odd[s:s + 1, :], both[64:, :], both[:64, :])

    def solve(t, parity):
        def finish(result):
            w, g = t // groups, t % groups
            for c in range(GIVEN):
                at = (c + 1) % GIVEN
                out_ref[pl.ds(g * 8 * given_pad + at * windows + w, 8, stride=given_pad), :] = result[c]

        return project(
            lambda k: coeffs[parity][8 * k:8 * k + 8, :],
            lambda: [arrived(t, c) for c in range(3)],
            lambda: (arrived(t, 3), arrived(t, 4)),
            finish)

    def interleave(rows, steps):
        done = 0
        for k, _ in enumerate(rows):
            while done < PROJECT_STEPS and done * 8 * LANES <= k * PROJECT_STEPS:
                next(steps, None)
                done += 1
        for _ in steps:
            pass

    for t in range(total):
        index_ref[8 * t:8 * t + 8, :] = arrived(t, 5).astype(jnp.int32) >> 1
    fetch(0, 0).start()
    fetch(1, 1).start()
    fetch(0, 0).wait()
    for _ in gather(0, 0):
        pass

    def pair(i, carry):
        t = 2 * i
        fetch(t + 1, 1).wait()
        fetch(t + 2, 0).start()
        interleave(gather(t + 1, 1), solve(t, 0))
        fetch(t + 2, 0).wait()
        fetch(t + 3, 1).start()
        interleave(gather(t + 2, 0), solve(t + 1, 1))
        return carry

    lax.fori_loop(0, total // 2 - 1, pair, 0)
    fetch(total - 1, 1).wait()
    interleave(gather(total - 1, 1), solve(total - 2, 0))
    for _ in solve(total - 1, 1):
        pass


def project_nodes(got, net, windows, given_pad):
    sources = got.shape[0]
    tiles = windows * sources
    return pl.pallas_call(
        functools.partial(project_kernel, sources, windows, given_pad),
        out_shape=jax.ShapeDtypeStruct((sources * given_pad, LANES), jnp.float32),
        in_specs=[pl.BlockSpec(memory_space=pltpu.VMEM)] * 2,
        out_specs=pl.BlockSpec(memory_space=pltpu.VMEM),
        scratch_shapes=[
            pltpu.VMEM((tiles, LANES), jnp.int32),
            pltpu.SMEM((8, LANES), jnp.int32),
            pltpu.SMEM((8, LANES), jnp.int32),
            pltpu.VMEM((8 * LANES, LANES), jnp.float32),
            pltpu.VMEM((64 * 8, LANES), jnp.float32),
            pltpu.VMEM((64 * 8, LANES), jnp.float32),
            pltpu.SemaphoreType.DMA((2,)),
        ],
        compiler_params=pltpu.CompilerParams(vmem_limit_bytes=30 * 2**20),
        name="project",
    )(got.reshape(sources * SENT * windows, LANES), net)


def return_kernel(owners, windows, given_pad, key_ref, first_smem, got_ref, out_ref):
    blocks = key_ref.shape[0]
    sub = iota((8, LANES), 0)

    def fetch(step, carry):
        for k in range(UNROLL):
            b = step * UNROLL + k
            key = jnp.broadcast_to(key_ref[pl.ds(b, 1), :], (8, LANES))
            lane = key & (LANES - 1)
            key = key >> 7
            rest = jnp.where(sub < 2, key - sub, -1)
            main = jnp.zeros((8, LANES), jnp.float32)
            last = jnp.zeros((8, LANES), jnp.float32)
            for o in range(owners):
                base = o * given_pad + first_smem[o, b]
                moved = take_lanes(got_ref[pl.ds(base, 8), :], lane)
                last = jnp.where(rest == 2 * o, moved, last)
                for step_over in range(2):
                    rows = got_ref[pl.ds(base + windows + step_over, 8, stride=windows), :]
                    main = jnp.where(key == 2 * o + step_over, take_lanes(rows, lane), main)
            at = pl.ds(pl.multiple_of(b * LANES, LANES), LANES)
            out_ref[0:8, at] = main
            out_ref[8:9, at] = jnp.sum(last, axis=0, keepdims=True)
        return carry

    lax.fori_loop(0, blocks // UNROLL, fetch, 0)


def return_nodes(key, first, got, windows, given_pad):
    owners, blocks = first.shape
    return pl.pallas_call(
        functools.partial(return_kernel, owners, windows, given_pad),
        out_shape=jax.ShapeDtypeStruct((GIVEN, blocks * LANES), jnp.float32),
        in_specs=[
            pl.BlockSpec(memory_space=pltpu.VMEM),
            pl.BlockSpec(memory_space=pltpu.SMEM),
            pl.BlockSpec(memory_space=pltpu.VMEM),
        ],
        out_specs=pl.BlockSpec(memory_space=pltpu.VMEM),
        compiler_params=pltpu.CompilerParams(vmem_limit_bytes=40 * 2**20),
        name="give_back",
    )(key, first, got.reshape(owners * given_pad, LANES))


def body(node_patch, node_span, start_grid, target, net):
    owners = lax.axis_size("bulk")
    windows = node_patch.shape[0] * 5 // 32 // LANES
    given_pad = round_up(GIVEN * windows + 1, 8)
    sent, key, first, net_rows = route(node_patch, node_span, start_grid, target, net, owners, windows)
    got = lax.all_to_all(sent, "bulk", split_axis=0, concat_axis=0, tiled=True)
    placed = project_nodes(got, net_rows, windows, given_pad)
    answered = lax.all_to_all(
        placed.reshape(owners, given_pad, LANES), "bulk", split_axis=0, concat_axis=0, tiled=True)
    return return_nodes(key, first, answered, windows, given_pad)


def solution(mesh):
    return jax.shard_map(
        body,
        mesh=mesh,
        in_specs=(
            P(("dom", "bulk")),
            P(("dom", "bulk")),
            P(None, ("dom", "bulk")),
            P(None, ("dom", "bulk")),
            P("bulk", None),
        ),
        out_specs=P(None, ("dom", "bulk")),
        check_vma=False,
    )
```

```python
import functools

import jax
import jax.numpy as jnp
from jax import lax
from jax.experimental import pallas as pl
from jax.experimental.pallas import tpu as pltpu
from jax.sharding import PartitionSpec as P

SPANS = 16
LEVELS = 16
ITERS = 4
LANES = 128
SENT = 6
GIVEN = 9
UNROLL = 16

damping = 0.1


def round_up(value, unit):
    return -(-value // unit) * unit


def iota(shape, dim):
    return lax.broadcasted_iota(jnp.int32, shape, dim)


def take_lanes(rows, lane):
    return jnp.take_along_axis(rows, lane, axis=1, mode="promise_in_bounds")


def route_kernel(owners, windows, patch_dev, patch_hbm, span_hbm, grid_hbm, target_hbm, net_hbm,
                 sent_ref, key_ref, first_ref, net_ref,
                 patch_ref, span_ref, grid_ref, target_ref,
                 code_ref, load_ref, slot_ref, first_smem, in_sem, net_sem, first_sem):
    copies = []
    for k, (source, to) in enumerate(
            ((patch_hbm, patch_ref), (span_hbm, span_ref), (grid_hbm, grid_ref), (target_hbm, target_ref))):
        copies.append(pltpu.make_async_copy(source, to, in_sem.at[k]))
        copies[-1].start()
    chunks = net_hbm.shape[1] // LANES
    patch_pad = net_ref.shape[0] // chunks
    loads = []
    for c in range(chunks):
        loads.append(pltpu.make_async_copy(
            net_hbm.at[:, pl.ds(c * LANES, LANES)], net_ref.at[pl.ds(c * patch_pad, patch_dev), :], net_sem.at[c]))
        loads[-1].start()
    slot_ref[...] = jnp.zeros_like(slot_ref)
    blocks = patch_ref.shape[0]
    copies[0].wait()
    patch = patch_ref[...]
    owner = jnp.zeros_like(patch)
    for o in range(1, owners):
        owner += (patch >= o * patch_dev).astype(jnp.int32)

    lane = iota((LANES, LANES), 1)
    sub = iota((LANES, LANES), 0)
    upto = (sub <= lane).astype(jnp.bfloat16)
    every = jnp.ones((LANES, LANES), jnp.bfloat16)
    counter = jnp.concatenate([upto, every], axis=1)
    earlier = (iota((blocks, blocks), 1) < iota((blocks, blocks), 0)).astype(jnp.bfloat16)
    blane = iota((blocks, LANES), 1)
    diagonal = iota((blocks, blocks), 0) == iota((blocks, blocks), 1)

    key = jnp.zeros_like(patch)
    for o in range(owners):
        mine = owner == o
        mask = mine.astype(jnp.bfloat16)
        counts = jnp.dot(mask, counter, preferred_element_type=jnp.float32)
        total = counts[:, LANES:]
        offset = jnp.dot(earlier, total.astype(jnp.bfloat16), preferred_element_type=jnp.float32).astype(jnp.int32)
        before = counts[:, :LANES].astype(jnp.int32) - mine.astype(jnp.int32)
        total = total.astype(jnp.int32)
        edge = offset & (LANES - 1)
        key = jnp.where(mine, before + edge + 2 * LANES * o, key)
        first = jnp.sum(jnp.where(diagonal, offset.astype(jnp.float32), 0.0), axis=0, keepdims=True)
        first_ref[o:o + 1, :] = first.astype(jnp.int32) >> 7
        word = jnp.where(mine, blane + LANES * (blane - before), 0)
        for bit in range(7):
            moves = 1 << (7 + bit)
            coming = pltpu.roll(word, LANES - (1 << bit), 1)
            word = jnp.where((coming & moves) != 0, coming, jnp.where((word & moves) != 0, 0, word))
        rank = (blane - edge) & (LANES - 1)
        source = take_lanes(word & (LANES - 1), rank)
        valid = rank < total
        code_ref[o * blocks:(o + 1) * blocks, :] = source + jnp.where(valid, jnp.where(blane >= edge, 128, 256), 0)

    key_ref[...] = key
    copy = pltpu.make_async_copy(first_ref, first_smem, first_sem)
    copy.start()
    for waiting in copies[1:]:
        waiting.wait()
    span = span_ref[...]
    row = (2 * ((span >> 1) * patch_pad + patch - owner * patch_dev) + (span & 1)).astype(jnp.float32)
    for b in range(blocks):
        load_ref[8 * b:8 * b + 3, :] = target_ref[:, b * LANES:(b + 1) * LANES]
        load_ref[8 * b + 3:8 * b + 5, :] = (grid_ref[:, b * LANES:(b + 1) * LANES].astype(jnp.float32) + 0.5) * (1.0 / LEVELS)
        load_ref[8 * b + 5:8 * b + 6, :] = row[b:b + 1, :]
    copy.wait()

    def place(step, carry):
        for k in range(UNROLL):
            b = step * UNROLL + k
            load = load_ref[pl.ds(pl.multiple_of(8 * b, 8), 8), :]
            for o in range(owners):
                code = jnp.broadcast_to(code_ref[pl.ds(o * blocks + b, 1), :], (8, LANES))
                moved = take_lanes(load, code & (LANES - 1))
                base = pl.multiple_of((o * (windows + 1) + first_smem[o, b]) * 8, 8)
                pltpu.store(slot_ref.at[pl.ds(base, 8), :], moved, mask=(code & 128) != 0)
                pltpu.store(slot_ref.at[pl.ds(base + 8, 8), :], moved, mask=(code & 256) != 0)
        return carry

    lax.fori_loop(0, blocks // UNROLL, place, 0)

    for o in range(owners):
        for c in range(SENT):
            for w in range(0, windows, 8):
                size = min(8, windows - w)
                rows = slot_ref[pl.ds((o * (windows + 1) + w) * 8 + c, size, stride=8), :]
                sent_ref[o, c * windows + w:c * windows + w + size, :] = rows
    for waiting in loads:
        waiting.wait()


def route(node_patch, node_span, start_grid, target, net, owners, windows):
    nodes = node_patch.shape[0]
    blocks = nodes // LANES
    patch_dev = net.shape[0]
    chunks = net.shape[1] // LANES
    patch_pad = round_up(patch_dev, 8)
    return pl.pallas_call(
        functools.partial(route_kernel, owners, windows, patch_dev),
        out_shape=(
            jax.ShapeDtypeStruct((owners, SENT * windows, LANES), jnp.float32),
            jax.ShapeDtypeStruct((blocks, LANES), jnp.int32),
            jax.ShapeDtypeStruct((owners, blocks), jnp.int32),
            jax.ShapeDtypeStruct((chunks * patch_pad, LANES), jnp.float32),
        ),
        in_specs=[pl.BlockSpec(memory_space=pltpu.HBM)] * 5,
        out_specs=[pl.BlockSpec(memory_space=pltpu.VMEM)] * 4,
        scratch_shapes=[
            pltpu.VMEM((blocks, LANES), jnp.int32),
            pltpu.VMEM((blocks, LANES), jnp.int32),
            pltpu.VMEM(start_grid.shape, jnp.int32),
            pltpu.VMEM(target.shape, jnp.float32),
            pltpu.VMEM((owners * blocks, LANES), jnp.int32),
            pltpu.VMEM((8 * blocks, LANES), jnp.float32),
            pltpu.VMEM((owners * (windows + 1) * 8, LANES), jnp.float32),
            pltpu.SMEM((owners, blocks), jnp.int32),
            pltpu.SemaphoreType.DMA((4,)),
            pltpu.SemaphoreType.DMA((chunks,)),
            pltpu.SemaphoreType.DMA,
        ],
        compiler_params=pltpu.CompilerParams(vmem_limit_bytes=16 * 2**20),
        name="route",
    )(*(pltpu.with_memory_space_constraint(x, pltpu.HBM) for x in (
        node_patch.reshape(blocks, LANES), node_span.reshape(blocks, LANES), start_grid, target, net)))


def bernstein(param):
    other = 1.0 - param
    square, cross, low = other * other, param * other, param * param
    value = (other * square, 3.0 * cross * other, 3.0 * param * cross, param * low)
    slope = (-3.0 * square, 3.0 * square - 6.0 * cross, 6.0 * cross - 3.0 * low, 3.0 * low)
    return value, slope


def weighted(weights, values):
    return (weights[0] * values[0] + weights[1] * values[1]) + (weights[2] * values[2] + weights[3] * values[3])


def surface(read, upar, vpar, answer):
    base_u, slope_u = bernstein(upar)
    base_v, slope_v = bernstein(vpar)
    yield
    point, along_u, along_v = [], [], []
    for c in range(4):
        mixed, mixed_u = [], []
        for j in range(4):
            column = [read(c * 16 + i * 4 + j) for i in range(4)]
            mixed.append(weighted(base_u, column))
            mixed_u.append(weighted(slope_u, column))
            yield
        point.append(weighted(base_v, mixed))
        along_u.append(weighted(base_v, mixed_u))
        along_v.append(weighted(slope_v, mixed))
        yield
    inverse = 1.0 / point[3]
    position = [point[c] * inverse for c in range(3)]
    yield
    tangent_u = [(along_u[c] - position[c] * along_u[3]) * inverse for c in range(3)]
    tangent_v = [(along_v[c] - position[c] * along_v[3]) * inverse for c in range(3)]
    yield
    answer.extend((position, tangent_u, tangent_v))


def inner(left, right):
    return left[0] * right[0] + left[1] * right[1] + left[2] * right[2]


def project(read, goal, start, finish):
    upar, vpar = start()
    goal = goal()
    for _ in range(ITERS):
        answer = []
        yield from surface(read, upar, vpar, answer)
        position, tangent_u, tangent_v = answer
        miss = [position[c] - goal[c] for c in range(3)]
        grad_u = inner(tangent_u, miss)
        grad_v = inner(tangent_v, miss)
        yield
        h_uu = inner(tangent_u, tangent_u) + damping
        h_vv = inner(tangent_v, tangent_v) + damping
        h_uv = inner(tangent_u, tangent_v)
        yield
        inverse = 1.0 / (h_uu * h_vv - h_uv * h_uv)
        upar = jnp.clip(upar - (h_vv * grad_u - h_uv * grad_v) * inverse, 0.0, 1.0)
        vpar = jnp.clip(vpar - (h_uu * grad_v - h_uv * grad_u) * inverse, 0.0, 1.0)
        yield
    answer = []
    yield from surface(read, upar, vpar, answer)
    finish(answer[0] + answer[1] + answer[2])


PROJECT_STEPS = ITERS * 27 + 25


def project_kernel(sources, windows, given_pad, got_ref, net_ref, out_ref,
                   index_ref, index_0, index_1, index_2, index_3, tile_even, tile_odd, coeff_even, coeff_odd, index_sem):
    groups = sources // 8
    sent = SENT * windows
    total = windows * groups
    indices = (index_0, index_1, index_2, index_3)
    tiles, coeffs = (tile_even, tile_odd), (coeff_even, coeff_odd)
    depth = len(indices)

    def arrived(t, c):
        w, g = t // groups, t % groups
        return got_ref[pl.ds(g * 8 * sent + c * windows + w, 8, stride=sent), :]

    def fetch(t, k):
        return pltpu.make_async_copy(
            index_ref.at[pl.ds(pl.multiple_of(8 * t, 8), 8), :], indices[k % depth], index_sem.at[k % depth])

    def gather(k):
        index, tile = indices[k % depth], tiles[k % 2]
        for s in range(8):
            for i in range(LANES):
                tile[s * LANES + i:s * LANES + i + 1, :] = net_ref[pl.ds(index[s, i], 1), :]
                yield

    def turn(t, k):
        tile, coeff = tiles[k % 2], coeffs[k % 2]
        odd = (arrived(t, 5).astype(jnp.int32) & 1) == 1
        for s in range(8):
            both = tile[s * LANES:(s + 1) * LANES, :].T
            coeff[pl.ds(s, 64, stride=8), :] = jnp.where(odd[s:s + 1, :], both[64:, :], both[:64, :])
            yield

    def solve(t, k):
        def finish(result):
            w, g = t // groups, t % groups
            for c in range(GIVEN):
                at = (c + 1) % GIVEN
                out_ref[pl.ds(g * 8 * given_pad + at * windows + w, 8, stride=given_pad), :] = result[c]

        return project(
            lambda e: coeffs[k % 2][8 * e:8 * e + 8, :],
            lambda: [arrived(t, c) for c in range(3)],
            lambda: (arrived(t, 3), arrived(t, 4)),
            finish)

    def interleave(*works):
        order = sorted(((at + 0.5) / size, k) for k, (_, size) in enumerate(works) for at in range(size))
        for _, k in order:
            next(works[k][0], None)
        for work, _ in works:
            for _ in work:
                pass

    def gathering(k):
        return gather(k), 8 * LANES

    def turning(t, k):
        return turn(t, k), 8

    def solving(t, k):
        return solve(t, k), PROJECT_STEPS

    for t in range(total):
        index_ref[8 * t:8 * t + 8, :] = arrived(t, 5).astype(jnp.int32) >> 1
        if t < depth:
            fetch(t, t).start()
    index_ref[8 * total:8 * total + 8, :] = jnp.zeros((8, LANES), jnp.int32)
    fetch(0, 0).wait()
    interleave(gathering(0))
    fetch(1, 1).wait()
    fetch(depth, depth).start()
    interleave(gathering(1), turning(0, 0))

    def steps(i, carry):
        for k in range(depth):
            t = depth * i + k
            fetch(t + 2, k + 2).wait()
            fetch(t + depth + 1, k + 1).start()
            interleave(gathering(k + 2), turning(t + 1, k + 1), solving(t, k))
        return carry

    lax.fori_loop(0, total // depth - 1, steps, 0)
    for t in range(total - depth, total):
        if t + 2 < total:
            fetch(t + 2, t + 2).wait()
            interleave(gathering(t + 2), turning(t + 1, t + 1), solving(t, t))
        elif t + 1 < total:
            interleave(turning(t + 1, t + 1), solving(t, t))
        else:
            interleave(solving(t, t))
    fetch(total, total).wait()


def project_nodes(got, net, windows, given_pad):
    sources = got.shape[0]
    tiles = windows * sources
    return pl.pallas_call(
        functools.partial(project_kernel, sources, windows, given_pad),
        out_shape=jax.ShapeDtypeStruct((sources * given_pad, LANES), jnp.float32),
        in_specs=[pl.BlockSpec(memory_space=pltpu.VMEM)] * 2,
        out_specs=pl.BlockSpec(memory_space=pltpu.VMEM),
        scratch_shapes=[
            pltpu.VMEM((tiles + 8, LANES), jnp.int32),
            pltpu.SMEM((8, LANES), jnp.int32),
            pltpu.SMEM((8, LANES), jnp.int32),
            pltpu.SMEM((8, LANES), jnp.int32),
            pltpu.SMEM((8, LANES), jnp.int32),
            pltpu.VMEM((8 * LANES, LANES), jnp.float32),
            pltpu.VMEM((8 * LANES, LANES), jnp.float32),
            pltpu.VMEM((64 * 8, LANES), jnp.float32),
            pltpu.VMEM((64 * 8, LANES), jnp.float32),
            pltpu.SemaphoreType.DMA((4,)),
        ],
        compiler_params=pltpu.CompilerParams(vmem_limit_bytes=24 * 2**20),
        name="project",
    )(got.reshape(sources * SENT * windows, LANES), net)


def return_kernel(owners, windows, given_pad, key_ref, first_smem, got_ref, out_ref):
    blocks = key_ref.shape[0]
    sub = iota((8, LANES), 0)

    def fetch(step, carry):
        for k in range(UNROLL):
            b = step * UNROLL + k
            key = jnp.broadcast_to(key_ref[pl.ds(b, 1), :], (8, LANES))
            lane = key & (LANES - 1)
            key = key >> 7
            rest = jnp.where(sub < 2, key - sub, -1)
            main = jnp.zeros((8, LANES), jnp.float32)
            last = jnp.zeros((8, LANES), jnp.float32)
            for o in range(owners):
                base = o * given_pad + first_smem[o, b]
                moved = take_lanes(got_ref[pl.ds(base, 8), :], lane)
                last = jnp.where(rest == 2 * o, moved, last)
                for step_over in range(2):
                    rows = got_ref[pl.ds(base + windows + step_over, 8, stride=windows), :]
                    main = jnp.where(key == 2 * o + step_over, take_lanes(rows, lane), main)
            at = pl.ds(pl.multiple_of(b * LANES, LANES), LANES)
            out_ref[0:8, at] = main
            out_ref[8:9, at] = jnp.sum(last, axis=0, keepdims=True)
        return carry

    lax.fori_loop(0, blocks // UNROLL, fetch, 0)


def return_nodes(key, first, got, windows, given_pad):
    owners, blocks = first.shape
    return pl.pallas_call(
        functools.partial(return_kernel, owners, windows, given_pad),
        out_shape=jax.ShapeDtypeStruct((GIVEN, blocks * LANES), jnp.float32),
        in_specs=[
            pl.BlockSpec(memory_space=pltpu.VMEM),
            pl.BlockSpec(memory_space=pltpu.SMEM),
            pl.BlockSpec(memory_space=pltpu.VMEM),
        ],
        out_specs=pl.BlockSpec(memory_space=pltpu.VMEM),
        compiler_params=pltpu.CompilerParams(vmem_limit_bytes=16 * 2**20),
        name="give_back",
    )(key, first, got.reshape(owners * given_pad, LANES))


def body(node_patch, node_span, start_grid, target, net):
    owners = lax.axis_size("bulk")
    windows = node_patch.shape[0] * 5 // 32 // LANES
    given_pad = round_up(GIVEN * windows + 1, 8)
    sent, key, first, net_rows = route(node_patch, node_span, start_grid, target, net, owners, windows)
    got = lax.all_to_all(sent, "bulk", split_axis=0, concat_axis=0, tiled=True)
    placed = project_nodes(got, net_rows, windows, given_pad)
    answered = lax.all_to_all(
        placed.reshape(owners, given_pad, LANES), "bulk", split_axis=0, concat_axis=0, tiled=True)
    return return_nodes(key, first, answered, windows, given_pad)


def solution(mesh):
    return jax.shard_map(
        body,
        mesh=mesh,
        in_specs=(
            P(("dom", "bulk")),
            P(("dom", "bulk")),
            P(None, ("dom", "bulk")),
            P(None, ("dom", "bulk")),
            P("bulk", None),
        ),
        out_specs=P(None, ("dom", "bulk")),
        check_vma=False,
    )
```

```python
import functools

import jax
import jax.numpy as jnp
from jax import lax
from jax.experimental import pallas as pl
from jax.experimental.pallas import tpu as pltpu
from jax.sharding import PartitionSpec as P

SPANS = 16
LEVELS = 16
ITERS = 4
LANES = 128
SENT = 6
GIVEN = 9
UNROLL = 16

damping = 0.1


def round_up(value, unit):
    return -(-value // unit) * unit


def iota(shape, dim):
    return lax.broadcasted_iota(jnp.int32, shape, dim)


def take_lanes(rows, lane):
    return jnp.take_along_axis(rows, lane, axis=1, mode="promise_in_bounds")


def route_kernel(owners, windows, patch_dev, patch_hbm, span_hbm, grid_hbm, target_hbm, net_hbm,
                 *refs):
    sent_refs = refs[:owners // 2]
    (key_ref, first_ref, net_ref, patch_ref, span_ref, grid_ref, target_ref,
     code_ref, load_ref, slot_ref, first_smem, in_sem, net_sem, first_sem) = refs[owners // 2:]
    me = lax.axis_index("bulk")
    copies = []
    for k, (source, to) in enumerate(
            ((patch_hbm, patch_ref), (span_hbm, span_ref), (grid_hbm, grid_ref), (target_hbm, target_ref))):
        copies.append(pltpu.make_async_copy(source, to, in_sem.at[k]))
        copies[-1].start()
    chunks = net_hbm.shape[1] // LANES
    patch_pad = net_ref.shape[0] // (2 * chunks)
    loads = []
    for c in range(chunks):
        loads.append(pltpu.make_async_copy(
            net_hbm.at[:, pl.ds(c * LANES, LANES)], net_ref.at[pl.ds(c * patch_pad, patch_dev), :], net_sem.at[c]))
        loads[-1].start()
    slot_ref[...] = jnp.zeros_like(slot_ref)
    blocks = patch_ref.shape[0]
    copies[0].wait()
    patch = patch_ref[...]
    owner = jnp.zeros_like(patch)
    for o in range(1, owners):
        owner += (patch >= o * patch_dev).astype(jnp.int32)
    local = patch - owner * patch_dev
    owner = owner ^ me

    lane = iota((LANES, LANES), 1)
    sub = iota((LANES, LANES), 0)
    upto = (sub <= lane).astype(jnp.bfloat16)
    every = jnp.ones((LANES, LANES), jnp.bfloat16)
    counter = jnp.concatenate([upto, every], axis=1)
    earlier = (iota((blocks, blocks), 1) < iota((blocks, blocks), 0)).astype(jnp.bfloat16)
    blane = iota((blocks, LANES), 1)
    diagonal = iota((blocks, blocks), 0) == iota((blocks, blocks), 1)

    key = jnp.zeros_like(patch)
    found = []
    for x in range(owners):
        mine = owner == x
        counts = jnp.dot(mine.astype(jnp.bfloat16), counter, preferred_element_type=jnp.float32)
        total = counts[:, LANES:]
        offset = jnp.dot(earlier, total.astype(jnp.bfloat16), preferred_element_type=jnp.float32)
        first = jnp.sum(jnp.where(diagonal, offset, 0.0), axis=0, keepdims=True)
        first_ref[x:x + 1, :] = first.astype(jnp.int32) >> 7
        before = counts[:, :LANES].astype(jnp.int32) - mine.astype(jnp.int32)
        edge = offset.astype(jnp.int32) & (LANES - 1)
        key = jnp.where(mine, before + edge + 2 * LANES * x, key)
        found.append((mine, before, edge, total.astype(jnp.int32)))
    copy = pltpu.make_async_copy(first_ref, first_smem, first_sem)
    copy.start()
    for x in range(owners):
        mine, before, edge, total = found[x]
        word = jnp.where(mine, blane + LANES * (blane - before), 0)
        for bit in range(7):
            moves = 1 << (7 + bit)
            coming = pltpu.roll(word, LANES - (1 << bit), 1)
            word = jnp.where((coming & moves) != 0, coming, jnp.where((word & moves) != 0, 0, word))
        rank = (blane - edge) & (LANES - 1)
        source = take_lanes(word & (LANES - 1), rank)
        valid = rank < total
        code_ref[x * blocks:(x + 1) * blocks, :] = source + jnp.where(valid, jnp.where(blane >= edge, 128, 256), 0)

    key_ref[...] = key
    for waiting in copies[1:]:
        waiting.wait()
    span = span_ref[...]
    row = (2 * ((span >> 1) * patch_pad + local) + (span & 1)).astype(jnp.float32)
    for b in range(blocks):
        load_ref[8 * b:8 * b + 3, :] = target_ref[:, b * LANES:(b + 1) * LANES]
        load_ref[8 * b + 3:8 * b + 5, :] = (grid_ref[:, b * LANES:(b + 1) * LANES].astype(jnp.float32) + 0.5) * (1.0 / LEVELS)
        load_ref[8 * b + 5:8 * b + 6, :] = row[b:b + 1, :]
    copy.wait()

    def place(step, carry):
        for k in range(UNROLL):
            b = step * UNROLL + k
            load = load_ref[pl.ds(pl.multiple_of(8 * b, 8), 8), :]
            for o in range(owners):
                code = jnp.broadcast_to(code_ref[pl.ds(o * blocks + b, 1), :], (8, LANES))
                moved = take_lanes(load, code & (LANES - 1))
                base = pl.multiple_of((o * (windows + 1) + first_smem[o, b]) * 8, 8)
                pltpu.store(slot_ref.at[pl.ds(base, 8), :], moved, mask=(code & 128) != 0)
                pltpu.store(slot_ref.at[pl.ds(base + 8, 8), :], moved, mask=(code & 256) != 0)
        return carry

    lax.fori_loop(0, blocks // UNROLL, place, 0)

    for x in range(owners):
        for c in range(SENT):
            for w in range(0, windows, 8):
                size = min(8, windows - w)
                rows = slot_ref[pl.ds((x * (windows + 1) + w) * 8 + c, size, stride=8), :]
                at = ((x % 2) * SENT + c) * windows + w
                sent_refs[x // 2][at:at + size, :] = rows
    for waiting in loads:
        waiting.wait()


def route(node_patch, node_span, start_grid, target, net, owners, windows):
    nodes = node_patch.shape[0]
    blocks = nodes // LANES
    patch_dev = net.shape[0]
    chunks = net.shape[1] // LANES
    patch_pad = round_up(patch_dev, 8)
    return pl.pallas_call(
        functools.partial(route_kernel, owners, windows, patch_dev),
        out_shape=(
            *[jax.ShapeDtypeStruct((2 * SENT * windows, LANES), jnp.float32)] * (owners // 2),
            jax.ShapeDtypeStruct((blocks, LANES), jnp.int32),
            jax.ShapeDtypeStruct((owners, blocks), jnp.int32),
            jax.ShapeDtypeStruct((2 * chunks * patch_pad, LANES), jnp.float32),
        ),
        in_specs=[pl.BlockSpec(memory_space=pltpu.HBM)] * 5,
        out_specs=[pl.BlockSpec(memory_space=pltpu.VMEM)] * (owners // 2 + 3),
        scratch_shapes=[
            pltpu.VMEM((blocks, LANES), jnp.int32),
            pltpu.VMEM((blocks, LANES), jnp.int32),
            pltpu.VMEM(start_grid.shape, jnp.int32),
            pltpu.VMEM(target.shape, jnp.float32),
            pltpu.VMEM((owners * blocks, LANES), jnp.int32),
            pltpu.VMEM((8 * blocks, LANES), jnp.float32),
            pltpu.VMEM((owners * (windows + 1) * 8, LANES), jnp.float32),
            pltpu.SMEM((owners, blocks), jnp.int32),
            pltpu.SemaphoreType.DMA((4,)),
            pltpu.SemaphoreType.DMA((chunks,)),
            pltpu.SemaphoreType.DMA,
        ],
        compiler_params=pltpu.CompilerParams(vmem_limit_bytes=16 * 2**20),
        name="route",
    )(*(pltpu.with_memory_space_constraint(x, pltpu.HBM) for x in (
        node_patch.reshape(blocks, LANES), node_span.reshape(blocks, LANES), start_grid, target, net)))


def bernstein(param):
    other = 1.0 - param
    square, cross, low = other * other, param * other, param * param
    value = (other * square, 3.0 * cross * other, 3.0 * param * cross, param * low)
    slope = (-3.0 * square, 3.0 * square - 6.0 * cross, 6.0 * cross - 3.0 * low, 3.0 * low)
    return value, slope


def weighted(weights, values):
    return (weights[0] * values[0] + weights[1] * values[1]) + (weights[2] * values[2] + weights[3] * values[3])


def surface(read, upar, vpar, answer):
    base_u, slope_u = bernstein(upar)
    base_v, slope_v = bernstein(vpar)
    yield
    point, along_u, along_v = [], [], []
    for c in range(4):
        mixed, mixed_u = [], []
        for j in range(4):
            column = [read(c * 16 + i * 4 + j) for i in range(4)]
            mixed.append(weighted(base_u, column))
            mixed_u.append(weighted(slope_u, column))
            yield
        point.append(weighted(base_v, mixed))
        along_u.append(weighted(base_v, mixed_u))
        along_v.append(weighted(slope_v, mixed))
        yield
    inverse = 1.0 / point[3]
    position = [point[c] * inverse for c in range(3)]
    yield
    tangent_u = [(along_u[c] - position[c] * along_u[3]) * inverse for c in range(3)]
    tangent_v = [(along_v[c] - position[c] * along_v[3]) * inverse for c in range(3)]
    yield
    answer.extend((position, tangent_u, tangent_v))


def inner(left, right):
    return left[0] * right[0] + left[1] * right[1] + left[2] * right[2]


def project(read, goal, start, finish):
    upar, vpar = start()
    goal = goal()
    for _ in range(ITERS):
        answer = []
        yield from surface(read, upar, vpar, answer)
        position, tangent_u, tangent_v = answer
        miss = [position[c] - goal[c] for c in range(3)]
        grad_u = inner(tangent_u, miss)
        grad_v = inner(tangent_v, miss)
        yield
        h_uu = inner(tangent_u, tangent_u) + damping
        h_vv = inner(tangent_v, tangent_v) + damping
        h_uv = inner(tangent_u, tangent_v)
        yield
        inverse = 1.0 / (h_uu * h_vv - h_uv * h_uv)
        upar = jnp.clip(upar - (h_vv * grad_u - h_uv * grad_v) * inverse, 0.0, 1.0)
        vpar = jnp.clip(vpar - (h_uu * grad_v - h_uv * grad_u) * inverse, 0.0, 1.0)
        yield
    answer = []
    yield from surface(read, upar, vpar, answer)
    finish(answer[0] + answer[1] + answer[2])


PROJECT_STEPS = ITERS * 27 + 25


def project_kernel(pairs, windows, given_pad, *refs):
    got_refs, (_, other_ref), out_refs = refs[:pairs], refs[pairs:pairs + 2], refs[pairs + 2:2 * pairs + 2]
    (net_ref, load_ref, index_ref, index_0, index_1, index_2, index_3,
     tile_even, tile_odd, coeff_even, coeff_odd, index_sem, net_sem) = refs[2 * pairs + 2:]
    per = 8 // pairs
    half = windows // per
    total = 2 * half
    rows = net_ref.shape[0] // 2
    indices = (index_0, index_1, index_2, index_3)
    tiles, coeffs = (tile_even, tile_odd), (coeff_even, coeff_odd)
    depth = len(indices)
    patches, chunks = other_ref.shape[0], other_ref.shape[1] // LANES
    patch_pad = rows // chunks

    def arrived(t, c):
        return load_ref[pl.ds(pl.multiple_of((t * SENT + c) * 8, 8), 8), :]

    def fetch(t, k):
        return pltpu.make_async_copy(
            index_ref.at[pl.ds(pl.multiple_of(8 * t, 8), 8), :], indices[k % depth], index_sem.at[k % depth])

    def partner(c):
        return pltpu.make_async_copy(
            other_ref.at[:, pl.ds(c * LANES, LANES)], net_ref.at[pl.ds(rows + c * patch_pad, patches), :], net_sem.at[c])

    def gather(k):
        index, tile = indices[k % depth], tiles[k % 2]
        for s in range(8):
            for i in range(LANES):
                tile[s * LANES + i:s * LANES + i + 1, :] = net_ref[pl.ds(index[s, i], 1), :]
                yield

    def turn(t, k):
        tile, coeff = tiles[k % 2], coeffs[k % 2]
        odd = (arrived(t, 5).astype(jnp.int32) & 1) == 1
        for s in range(8):
            both = tile[s * LANES:(s + 1) * LANES, :].T
            coeff[pl.ds(s, 64, stride=8), :] = jnp.where(odd[s:s + 1, :], both[64:, :], both[:64, :])
            yield

    def solve(t, k):
        def finish(result):
            base = t // half * given_pad + t % half * per
            for c in range(GIVEN):
                at = (c + 1) % GIVEN
                for j in range(pairs):
                    out_refs[j][pl.ds(base + at * windows, per), :] = result[c][j * per:(j + 1) * per, :]

        return project(
            lambda e: coeffs[k % 2][8 * e:8 * e + 8, :],
            lambda: [arrived(t, c) for c in range(3)],
            lambda: (arrived(t, 3), arrived(t, 4)),
            finish)

    def interleave(*works):
        order = sorted(((at + 0.5) / size, k) for k, (_, size) in enumerate(works) for at in range(size))
        for _, k in order:
            next(works[k][0], None)
        for work, _ in works:
            for _ in work:
                pass

    def gathering(k):
        return gather(k), 8 * LANES

    def turning(t, k):
        return turn(t, k), 8

    def solving(t, k):
        return solve(t, k), PROJECT_STEPS

    def collect(t, c):
        at = (t // half * SENT + c) * windows + t % half * per
        for j in range(pairs):
            to = (t * SENT + c) * 8 + j * per
            load_ref[to:to + per, :] = got_refs[j][at:at + per, :]

    for t in range(total):
        collect(t, SENT - 1)
        index_ref[8 * t:8 * t + 8, :] = (arrived(t, SENT - 1).astype(jnp.int32) >> 1) + t // half * rows
        if t < depth:
            fetch(t, t).start()
    for c in range(chunks):
        partner(c).start()
    for t in range(total):
        for c in range(SENT - 1):
            collect(t, c)
    index_ref[8 * total:8 * total + 8, :] = jnp.zeros((8, LANES), jnp.int32)
    fetch(0, 0).wait()
    interleave(gathering(0))
    fetch(1, 1).wait()
    fetch(depth, depth).start()
    interleave(gathering(1), turning(0, 0))

    def steps(i, carry):
        @pl.when(i == -(-(half - depth - 1) // depth))
        def _():
            for c in range(chunks):
                partner(c).wait()

        for k in range(depth):
            t = depth * i + k
            fetch(t + 2, k + 2).wait()
            fetch(t + depth + 1, k + 1).start()
            interleave(gathering(k + 2), turning(t + 1, k + 1), solving(t, k))
        return carry

    lax.fori_loop(0, total // depth - 1, steps, 0)
    for t in range(total - depth, total):
        if t + 2 < total:
            fetch(t + 2, t + 2).wait()
            interleave(gathering(t + 2), turning(t + 1, t + 1), solving(t, t))
        elif t + 1 < total:
            interleave(turning(t + 1, t + 1), solving(t, t))
        else:
            interleave(solving(t, t))
    fetch(total, total).wait()


def project_nodes(got, net_rows, other, windows, given_pad):
    pairs = len(got)
    chunks = other.shape[1] // LANES
    tiles = 2 * pairs * windows
    return pl.pallas_call(
        functools.partial(project_kernel, pairs, windows, given_pad),
        out_shape=(
            *[jax.ShapeDtypeStruct((2 * given_pad, LANES), jnp.float32)] * pairs,
            jax.ShapeDtypeStruct(net_rows.shape, jnp.float32),
        ),
        in_specs=[pl.BlockSpec(memory_space=pltpu.VMEM)] * (pairs + 1) + [pl.BlockSpec(memory_space=pl.ANY)],
        out_specs=[pl.BlockSpec(memory_space=pltpu.VMEM)] * (pairs + 1),
        input_output_aliases={pairs: pairs},
        scratch_shapes=[
            pltpu.VMEM((tiles * SENT, LANES), jnp.float32),
            pltpu.VMEM((tiles + 8, LANES), jnp.int32),
            pltpu.SMEM((8, LANES), jnp.int32),
            pltpu.SMEM((8, LANES), jnp.int32),
            pltpu.SMEM((8, LANES), jnp.int32),
            pltpu.SMEM((8, LANES), jnp.int32),
            pltpu.VMEM((8 * LANES, LANES), jnp.float32),
            pltpu.VMEM((8 * LANES, LANES), jnp.float32),
            pltpu.VMEM((64 * 8, LANES), jnp.float32),
            pltpu.VMEM((64 * 8, LANES), jnp.float32),
            pltpu.SemaphoreType.DMA((4,)),
            pltpu.SemaphoreType.DMA((chunks,)),
        ],
        compiler_params=pltpu.CompilerParams(vmem_limit_bytes=12 * 2**20),
        name="project",
    )(*got, net_rows, other)[:pairs]


def return_kernel(owners, windows, given_pad, key_ref, first_smem, *refs):
    got_refs, out_ref = refs[:-1], refs[-1]
    blocks = key_ref.shape[0]
    sub = iota((8, LANES), 0)

    def fetch(step, carry):
        for k in range(UNROLL):
            b = step * UNROLL + k
            key = jnp.broadcast_to(key_ref[pl.ds(b, 1), :], (8, LANES))
            lane = key & (LANES - 1)
            key = key >> 7
            rest = jnp.where(sub < 2, key - sub, -1)
            main = jnp.zeros((8, LANES), jnp.float32)
            last = jnp.zeros((8, LANES), jnp.float32)
            for x in range(owners):
                got_ref = got_refs[x // 2]
                base = (x % 2) * given_pad + first_smem[x, b]
                moved = take_lanes(got_ref[pl.ds(base, 8), :], lane)
                last = jnp.where(rest == 2 * x, moved, last)
                for step_over in range(2):
                    rows = got_ref[pl.ds(base + windows + step_over, 8, stride=windows), :]
                    main = jnp.where(key == 2 * x + step_over, take_lanes(rows, lane), main)
            at = pl.ds(pl.multiple_of(b * LANES, LANES), LANES)
            out_ref[0:8, at] = main
            out_ref[8:9, at] = jnp.sum(last, axis=0, keepdims=True)
        return carry

    lax.fori_loop(0, blocks // UNROLL, fetch, 0)


def return_nodes(key, first, got, windows, given_pad):
    owners, blocks = first.shape
    return pl.pallas_call(
        functools.partial(return_kernel, owners, windows, given_pad),
        out_shape=jax.ShapeDtypeStruct((GIVEN, blocks * LANES), jnp.float32),
        in_specs=[
            pl.BlockSpec(memory_space=pltpu.VMEM),
            pl.BlockSpec(memory_space=pltpu.SMEM),
        ] + [pl.BlockSpec(memory_space=pltpu.VMEM)] * len(got),
        out_specs=pl.BlockSpec(memory_space=pltpu.VMEM),
        compiler_params=pltpu.CompilerParams(vmem_limit_bytes=16 * 2**20),
        name="give_back",
    )(key, first, *got)


def body(node_patch, node_span, start_grid, target, net):
    owners = lax.axis_size("bulk")
    windows = node_patch.shape[0] * 5 // 32 // LANES
    given_pad = round_up(GIVEN * windows + 1, 8)
    def swap(value, distance):
        return lax.ppermute(value, "bulk", [(i, i ^ distance) for i in range(owners)])

    def swap_pairs(values):
        return [swap(value, 2 * j) if j else value for j, value in enumerate(values)]

    other = swap(net, 1)
    *sent, key, first, net_rows = route(node_patch, node_span, start_grid, target, net, owners, windows)
    placed = project_nodes(swap_pairs(sent), net_rows, other, windows, given_pad)
    return return_nodes(key, first, swap_pairs(placed), windows, given_pad)


def solution(mesh):
    return jax.shard_map(
        body,
        mesh=mesh,
        in_specs=(
            P(("dom", "bulk")),
            P(("dom", "bulk")),
            P(None, ("dom", "bulk")),
            P(None, ("dom", "bulk")),
            P("bulk", None),
        ),
        out_specs=P(None, ("dom", "bulk")),
        check_vma=False,
    )
```

```python
import functools

import jax
import jax.numpy as jnp
from jax import lax
from jax.experimental import pallas as pl
from jax.experimental.pallas import tpu as pltpu
from jax.sharding import PartitionSpec as P

SPANS = 16
LEVELS = 16
ITERS = 4
LANES = 128
SENT = 6
GIVEN = 9
UNROLL = 16

damping = 0.1


def round_up(value, unit):
    return -(-value // unit) * unit


def iota(shape, dim):
    return lax.broadcasted_iota(jnp.int32, shape, dim)


def take_lanes(rows, lane):
    return jnp.take_along_axis(rows, lane, axis=1, mode="promise_in_bounds")


def route_kernel(owners, windows, patch_dev, patch_hbm, span_hbm, grid_hbm, target_hbm, net_hbm,
                 *refs):
    sent_refs = refs[:owners // 2]
    (key_ref, first_ref, net_ref, patch_ref, span_ref, grid_ref, target_ref,
     code_ref, load_ref, slot_ref, first_smem, in_sem, net_sem, first_sem) = refs[owners // 2:]
    me = lax.axis_index("bulk")
    copies = []
    for k, (source, to) in enumerate(
            ((patch_hbm, patch_ref), (span_hbm, span_ref), (grid_hbm, grid_ref), (target_hbm, target_ref))):
        copies.append(pltpu.make_async_copy(source, to, in_sem.at[k]))
        copies[-1].start()
    chunks = net_hbm.shape[1] // LANES
    patch_pad = net_ref.shape[0] // (2 * chunks)
    loads = []
    for c in range(chunks):
        loads.append(pltpu.make_async_copy(
            net_hbm.at[:, pl.ds(c * LANES, LANES)], net_ref.at[pl.ds(c * patch_pad, patch_dev), :], net_sem.at[c]))
    for load in loads[:chunks // 2]:
        load.start()
    slot_ref[...] = jnp.zeros_like(slot_ref)
    blocks = patch_ref.shape[0]
    copies[0].wait()
    patch = patch_ref[...]
    owner = jnp.zeros_like(patch)
    for o in range(1, owners):
        owner += (patch >= o * patch_dev).astype(jnp.int32)
    local = patch - owner * patch_dev
    owner = owner ^ me

    lane = iota((LANES, LANES), 1)
    sub = iota((LANES, LANES), 0)
    upto = (sub <= lane).astype(jnp.bfloat16)
    every = jnp.ones((LANES, LANES), jnp.bfloat16)
    counter = jnp.concatenate([upto, every], axis=1)
    earlier = (iota((blocks, blocks), 1) < iota((blocks, blocks), 0)).astype(jnp.bfloat16)
    blane = iota((blocks, LANES), 1)
    diagonal = iota((blocks, blocks), 0) == iota((blocks, blocks), 1)

    key = jnp.zeros_like(patch)
    found = []
    for x in range(owners):
        mine = owner == x
        counts = jnp.dot(mine.astype(jnp.bfloat16), counter, preferred_element_type=jnp.float32)
        total = counts[:, LANES:]
        offset = jnp.dot(earlier, total.astype(jnp.bfloat16), preferred_element_type=jnp.float32)
        first = jnp.sum(jnp.where(diagonal, offset, 0.0), axis=0, keepdims=True)
        first_ref[x:x + 1, :] = first.astype(jnp.int32) >> 7
        before = counts[:, :LANES].astype(jnp.int32) - mine.astype(jnp.int32)
        edge = offset.astype(jnp.int32) & (LANES - 1)
        key = jnp.where(mine, before + edge + 2 * LANES * x, key)
        found.append((mine, before, edge, total.astype(jnp.int32)))
    copy = pltpu.make_async_copy(first_ref, first_smem, first_sem)
    copy.start()
    for load in loads[chunks // 2:]:
        load.start()
    for x in range(owners):
        mine, before, edge, total = found[x]
        word = jnp.where(mine, blane + LANES * (blane - before), 0)
        for bit in range(7):
            moves = 1 << (7 + bit)
            coming = pltpu.roll(word, LANES - (1 << bit), 1)
            word = jnp.where((coming & moves) != 0, coming, jnp.where((word & moves) != 0, 0, word))
        rank = (blane - edge) & (LANES - 1)
        source = take_lanes(word & (LANES - 1), rank)
        valid = rank < total
        code_ref[x * blocks:(x + 1) * blocks, :] = source + jnp.where(valid, jnp.where(blane >= edge, 128, 256), 0)

    key_ref[...] = key
    for waiting in copies[1:]:
        waiting.wait()
    span = span_ref[...]
    row = (2 * ((span >> 1) * patch_pad + local) + (span & 1)).astype(jnp.float32)
    for b in range(blocks):
        load_ref[8 * b:8 * b + 3, :] = target_ref[:, b * LANES:(b + 1) * LANES]
        load_ref[8 * b + 3:8 * b + 5, :] = (grid_ref[:, b * LANES:(b + 1) * LANES].astype(jnp.float32) + 0.5) * (1.0 / LEVELS)
        load_ref[8 * b + 5:8 * b + 6, :] = row[b:b + 1, :]
    copy.wait()

    def place(step, carry):
        for k in range(UNROLL):
            b = step * UNROLL + k
            load = load_ref[pl.ds(pl.multiple_of(8 * b, 8), 8), :]
            for o in range(owners):
                code = jnp.broadcast_to(code_ref[pl.ds(o * blocks + b, 1), :], (8, LANES))
                moved = take_lanes(load, code & (LANES - 1))
                base = pl.multiple_of((o * (windows + 1) + first_smem[o, b]) * 8, 8)
                pltpu.store(slot_ref.at[pl.ds(base, 8), :], moved, mask=(code & 128) != 0)
                pltpu.store(slot_ref.at[pl.ds(base + 8, 8), :], moved, mask=(code & 256) != 0)
        return carry

    lax.fori_loop(0, blocks // UNROLL, place, 0)

    for x in range(owners):
        for c in range(SENT):
            for w in range(0, windows, 8):
                size = min(8, windows - w)
                rows = slot_ref[pl.ds((x * (windows + 1) + w) * 8 + c, size, stride=8), :]
                at = ((x % 2) * SENT + c) * windows + w
                sent_refs[x // 2][at:at + size, :] = rows
    for waiting in loads:
        waiting.wait()


def route(node_patch, node_span, start_grid, target, net, owners, windows):
    nodes = node_patch.shape[0]
    blocks = nodes // LANES
    patch_dev = net.shape[0]
    chunks = net.shape[1] // LANES
    patch_pad = round_up(patch_dev, 8)
    return pl.pallas_call(
        functools.partial(route_kernel, owners, windows, patch_dev),
        out_shape=(
            *[jax.ShapeDtypeStruct((2 * SENT * windows, LANES), jnp.float32)] * (owners // 2),
            jax.ShapeDtypeStruct((blocks, LANES), jnp.int32),
            jax.ShapeDtypeStruct((owners, blocks), jnp.int32),
            jax.ShapeDtypeStruct((2 * chunks * patch_pad, LANES), jnp.float32),
        ),
        in_specs=[pl.BlockSpec(memory_space=pltpu.HBM)] * 5,
        out_specs=[pl.BlockSpec(memory_space=pltpu.VMEM)] * (owners // 2 + 3),
        scratch_shapes=[
            pltpu.VMEM((blocks, LANES), jnp.int32),
            pltpu.VMEM((blocks, LANES), jnp.int32),
            pltpu.VMEM(start_grid.shape, jnp.int32),
            pltpu.VMEM(target.shape, jnp.float32),
            pltpu.VMEM((owners * blocks, LANES), jnp.int32),
            pltpu.VMEM((8 * blocks, LANES), jnp.float32),
            pltpu.VMEM((owners * (windows + 1) * 8, LANES), jnp.float32),
            pltpu.SMEM((owners, blocks), jnp.int32),
            pltpu.SemaphoreType.DMA((4,)),
            pltpu.SemaphoreType.DMA((chunks,)),
            pltpu.SemaphoreType.DMA,
        ],
        compiler_params=pltpu.CompilerParams(vmem_limit_bytes=16 * 2**20),
        name="route",
    )(*(pltpu.with_memory_space_constraint(x, pltpu.HBM) for x in (
        node_patch.reshape(blocks, LANES), node_span.reshape(blocks, LANES), start_grid, target, net)))


def bernstein(param):
    other = 1.0 - param
    square, cross, low = other * other, param * other, param * param
    value = (other * square, 3.0 * cross * other, 3.0 * param * cross, param * low)
    slope = (-3.0 * square, 3.0 * square - 6.0 * cross, 6.0 * cross - 3.0 * low, 3.0 * low)
    return value, slope


def weighted(weights, values):
    return (weights[0] * values[0] + weights[1] * values[1]) + (weights[2] * values[2] + weights[3] * values[3])


def surface(read, upar, vpar, answer):
    base_u, slope_u = bernstein(upar)
    base_v, slope_v = bernstein(vpar)
    yield
    point, along_u, along_v = [], [], []
    for c in range(4):
        mixed, mixed_u = [], []
        for j in range(4):
            column = [read(c * 16 + i * 4 + j) for i in range(4)]
            mixed.append(weighted(base_u, column))
            mixed_u.append(weighted(slope_u, column))
            yield
        point.append(weighted(base_v, mixed))
        along_u.append(weighted(base_v, mixed_u))
        along_v.append(weighted(slope_v, mixed))
        yield
    inverse = 1.0 / point[3]
    position = [point[c] * inverse for c in range(3)]
    yield
    tangent_u = [(along_u[c] - position[c] * along_u[3]) * inverse for c in range(3)]
    tangent_v = [(along_v[c] - position[c] * along_v[3]) * inverse for c in range(3)]
    yield
    answer.extend((position, tangent_u, tangent_v))


def inner(left, right):
    return left[0] * right[0] + left[1] * right[1] + left[2] * right[2]


def project(read, goal, start, finish):
    upar, vpar = start()
    goal = goal()
    for _ in range(ITERS):
        answer = []
        yield from surface(read, upar, vpar, answer)
        position, tangent_u, tangent_v = answer
        miss = [position[c] - goal[c] for c in range(3)]
        grad_u = inner(tangent_u, miss)
        grad_v = inner(tangent_v, miss)
        yield
        h_uu = inner(tangent_u, tangent_u) + damping
        h_vv = inner(tangent_v, tangent_v) + damping
        h_uv = inner(tangent_u, tangent_v)
        yield
        inverse = 1.0 / (h_uu * h_vv - h_uv * h_uv)
        upar = jnp.clip(upar - (h_vv * grad_u - h_uv * grad_v) * inverse, 0.0, 1.0)
        vpar = jnp.clip(vpar - (h_uu * grad_v - h_uv * grad_u) * inverse, 0.0, 1.0)
        yield
    answer = []
    yield from surface(read, upar, vpar, answer)
    finish(answer[0] + answer[1] + answer[2])


PROJECT_STEPS = ITERS * 27 + 25


def project_kernel(pairs, windows, given_pad, *refs):
    got_refs, (_, other_ref), out_refs = refs[:pairs], refs[pairs:pairs + 2], refs[pairs + 2:2 * pairs + 2]
    (net_ref, load_ref, index_ref, index_0, index_1, index_2, index_3,
     tile_even, tile_odd, turn_even, turn_odd, coeff_ref, index_sem, net_sem) = refs[2 * pairs + 2:]
    per = 8 // pairs
    half = windows // per
    total = 2 * half
    rows = net_ref.shape[0] // 2
    indices = (index_0, index_1, index_2, index_3)
    tiles, turns = (tile_even, tile_odd), (turn_even, turn_odd)
    depth = len(indices)
    patches, chunks = other_ref.shape[0], other_ref.shape[1] // LANES
    patch_pad = rows // chunks

    def arrived(t, c):
        return load_ref[pl.ds(pl.multiple_of((t * SENT + c) * 8, 8), 8), :]

    def fetch(t, k):
        return pltpu.make_async_copy(
            index_ref.at[pl.ds(pl.multiple_of(8 * t, 8), 8), :], indices[k % depth], index_sem.at[k % depth])

    def partner(c):
        return pltpu.make_async_copy(
            other_ref.at[:, pl.ds(c * LANES, LANES)], net_ref.at[pl.ds(rows + c * patch_pad, patches), :], net_sem.at[c])

    def gather(k):
        index, tile = indices[k % depth], tiles[k % 2]
        for s in range(8):
            for i in range(LANES):
                tile[s * LANES + i:s * LANES + i + 1, :] = net_ref[pl.ds(index[s, i], 1), :]
                yield

    def turn(k):
        tile, turned = tiles[k % 2], turns[k % 2]
        for s in range(8):
            turned[pl.ds(s, LANES, stride=8), :] = tile[s * LANES:(s + 1) * LANES, :].T
            yield

    def solve(t, k):
        turned = turns[k % 2]
        odd = (arrived(t, SENT - 1).astype(jnp.int32) & 1) == 1
        kept = set()

        def read(e):
            at = slice(8 * e, 8 * e + 8)
            if e not in kept:
                kept.add(e)
                coeff_ref[at, :] = jnp.where(odd, turned[512 + 8 * e:520 + 8 * e, :], turned[at, :])
            return coeff_ref[at, :]

        def finish(result):
            base = t // half * given_pad + t % half * per
            for c in range(GIVEN):
                at = (c + 1) % GIVEN
                for j in range(pairs):
                    out_refs[j][pl.ds(base + at * windows, per), :] = result[c][j * per:(j + 1) * per, :]

        return project(
            read,
            lambda: [arrived(t, c) for c in range(3)],
            lambda: (arrived(t, 3), arrived(t, 4)),
            finish)

    def interleave(*works):
        order = sorted(((at + 0.5) / size, k) for k, (_, size) in enumerate(works) for at in range(size))
        for _, k in order:
            next(works[k][0], None)
        for work, _ in works:
            for _ in work:
                pass

    def gathering(k):
        return gather(k), 8 * LANES

    def turning(k):
        return turn(k), 8

    def solving(t, k):
        return solve(t, k), PROJECT_STEPS

    def collect(t, c):
        at = (t // half * SENT + c) * windows + t % half * per
        for j in range(pairs):
            to = (t * SENT + c) * 8 + j * per
            load_ref[to:to + per, :] = got_refs[j][at:at + per, :]

    for t in range(total):
        collect(t, SENT - 1)
        index_ref[8 * t:8 * t + 8, :] = (arrived(t, SENT - 1).astype(jnp.int32) >> 1) + t // half * rows
        if t < depth:
            fetch(t, t).start()
    for c in range(chunks):
        partner(c).start()
    for t in range(total):
        for c in range(SENT - 1):
            collect(t, c)
    index_ref[8 * total:8 * total + 16, :] = jnp.zeros((16, LANES), jnp.int32)
    fetch(0, 0).wait()
    interleave(gathering(0))
    fetch(depth, depth).start()
    fetch(1, 1).wait()
    interleave(gathering(1), turning(0))
    fetch(depth + 1, depth + 1).start()

    def steps(i, carry):
        @pl.when(i == -(-(half - depth - 1) // depth))
        def _():
            for c in range(chunks):
                partner(c).wait()

        for k in range(depth):
            t = depth * i + k
            fetch(t + 2, k + 2).wait()
            interleave(gathering(k + 2), turning(k + 1), solving(t, k))
            fetch(t + depth + 2, k + 2).start()
        return carry

    lax.fori_loop(0, total // depth - 1, steps, 0)
    for t in range(total - depth, total):
        if t + 2 < total:
            fetch(t + 2, t + 2).wait()
            interleave(gathering(t + 2), turning(t + 1), solving(t, t))
        elif t + 1 < total:
            interleave(turning(t + 1), solving(t, t))
        else:
            interleave(solving(t, t))
    for t in (total, total + 1):
        fetch(t, t).wait()


def project_nodes(got, net_rows, other, windows, given_pad):
    pairs = len(got)
    chunks = other.shape[1] // LANES
    tiles = 2 * pairs * windows
    return pl.pallas_call(
        functools.partial(project_kernel, pairs, windows, given_pad),
        out_shape=(
            *[jax.ShapeDtypeStruct((2 * given_pad, LANES), jnp.float32)] * pairs,
            jax.ShapeDtypeStruct(net_rows.shape, jnp.float32),
        ),
        in_specs=[pl.BlockSpec(memory_space=pltpu.VMEM)] * (pairs + 1) + [pl.BlockSpec(memory_space=pl.ANY)],
        out_specs=[pl.BlockSpec(memory_space=pltpu.VMEM)] * (pairs + 1),
        input_output_aliases={pairs: pairs},
        scratch_shapes=[
            pltpu.VMEM((tiles * SENT, LANES), jnp.float32),
            pltpu.VMEM((tiles + 16, LANES), jnp.int32),
            pltpu.SMEM((8, LANES), jnp.int32),
            pltpu.SMEM((8, LANES), jnp.int32),
            pltpu.SMEM((8, LANES), jnp.int32),
            pltpu.SMEM((8, LANES), jnp.int32),
            pltpu.VMEM((8 * LANES, LANES), jnp.float32),
            pltpu.VMEM((8 * LANES, LANES), jnp.float32),
            pltpu.VMEM((8 * LANES, LANES), jnp.float32),
            pltpu.VMEM((8 * LANES, LANES), jnp.float32),
            pltpu.VMEM((64 * 8, LANES), jnp.float32),
            pltpu.SemaphoreType.DMA((4,)),
            pltpu.SemaphoreType.DMA((chunks,)),
        ],
        compiler_params=pltpu.CompilerParams(vmem_limit_bytes=12 * 2**20),
        name="project",
    )(*got, net_rows, other)[:pairs]


def return_kernel(owners, windows, given_pad, key_ref, first_smem, *refs):
    got_refs, (out_hbm, out_ref, out_sem) = refs[:-3], refs[-3:]
    blocks = key_ref.shape[0]
    sub = iota((8, LANES), 0)

    def fetch(step, carry):
        for k in range(UNROLL):
            b = step * UNROLL + k
            key = jnp.broadcast_to(key_ref[pl.ds(b, 1), :], (8, LANES))
            lane = key & (LANES - 1)
            key = key >> 7
            rest = jnp.where(sub < 2, key - sub, -1)
            main = jnp.zeros((8, LANES), jnp.float32)
            last = jnp.zeros((8, LANES), jnp.float32)
            for x in range(owners):
                got_ref = got_refs[x // 2]
                base = (x % 2) * given_pad + first_smem[x, b]
                moved = take_lanes(got_ref[pl.ds(base, 8), :], lane)
                last = jnp.where(rest == 2 * x, moved, last)
                for step_over in range(2):
                    rows = got_ref[pl.ds(base + windows + step_over, 8, stride=windows), :]
                    main = jnp.where(key == 2 * x + step_over, take_lanes(rows, lane), main)
            at = pl.ds(pl.multiple_of(b * LANES, LANES), LANES)
            out_ref[0:8, at] = main
            out_ref[8:9, at] = jnp.sum(last, axis=0, keepdims=True)
        return carry

    trips = blocks // UNROLL
    parts = 4 if trips % 4 == 0 else 1
    copies = []
    for part in range(parts):
        lax.fori_loop(part * trips // parts, (part + 1) * trips // parts, fetch, 0)
        at = pl.ds(part * blocks // parts * LANES, blocks // parts * LANES)
        copies.append(pltpu.make_async_copy(out_ref.at[:, at], out_hbm.at[:, at], out_sem.at[part]))
        copies[-1].start()
    for copy in copies:
        copy.wait()


def return_nodes(key, first, got, windows, given_pad):
    owners, blocks = first.shape
    return pl.pallas_call(
        functools.partial(return_kernel, owners, windows, given_pad),
        out_shape=jax.ShapeDtypeStruct((GIVEN, blocks * LANES), jnp.float32),
        in_specs=[
            pl.BlockSpec(memory_space=pltpu.VMEM),
            pl.BlockSpec(memory_space=pltpu.SMEM),
        ] + [pl.BlockSpec(memory_space=pltpu.VMEM)] * len(got),
        out_specs=pl.BlockSpec(memory_space=pltpu.HBM),
        scratch_shapes=[pltpu.VMEM((GIVEN, blocks * LANES), jnp.float32), pltpu.SemaphoreType.DMA((4,))],
        compiler_params=pltpu.CompilerParams(vmem_limit_bytes=16 * 2**20),
        name="give_back",
    )(key, first, *got)


def body(node_patch, node_span, start_grid, target, net):
    owners = lax.axis_size("bulk")
    windows = node_patch.shape[0] * 5 // 32 // LANES
    given_pad = round_up(GIVEN * windows + 1, 8)
    def swap(value, distance):
        return lax.ppermute(value, "bulk", [(i, i ^ distance) for i in range(owners)])

    def swap_pairs(values):
        return [swap(value, 2 * j) if j else value for j, value in enumerate(values)]

    other = swap(net, 1)
    *sent, key, first, net_rows = route(node_patch, node_span, start_grid, target, net, owners, windows)
    placed = project_nodes(swap_pairs(sent), net_rows, other, windows, given_pad)
    return return_nodes(key, first, swap_pairs(placed), windows, given_pad)


def solution(mesh):
    return jax.shard_map(
        body,
        mesh=mesh,
        in_specs=(
            P(("dom", "bulk")),
            P(("dom", "bulk")),
            P(None, ("dom", "bulk")),
            P(None, ("dom", "bulk")),
            P("bulk", None),
        ),
        out_specs=P(None, ("dom", "bulk")),
        check_vma=False,
    )
```

```python
import functools

import jax
import jax.numpy as jnp
from jax import lax
from jax.experimental import pallas as pl
from jax.experimental.pallas import tpu as pltpu
from jax.sharding import PartitionSpec as P

SPANS = 16
LEVELS = 16
ITERS = 4
LANES = 128
SENT = 6
GIVEN = 9
UNROLL = 32

damping = 0.1


def round_up(value, unit):
    return -(-value // unit) * unit


def iota(shape, dim):
    return lax.broadcasted_iota(jnp.int32, shape, dim)


def take_lanes(rows, lane):
    return jnp.take_along_axis(rows, lane, axis=1, mode="promise_in_bounds")


def route_kernel(owners, windows, patch_dev, patch_hbm, span_hbm, grid_hbm, target_hbm, net_hbm,
                 *refs):
    sent_refs = refs[:owners // 2]
    (key_ref, first_ref, net_ref, patch_ref, span_ref, grid_ref, target_ref,
     code_ref, load_ref, slot_ref, base_ref, base_smem, in_sem, net_sem, base_sem) = refs[owners // 2:]
    me = lax.axis_index("bulk")
    copies = []
    for k, (source, to) in enumerate(
            ((patch_hbm, patch_ref), (span_hbm, span_ref), (grid_hbm, grid_ref), (target_hbm, target_ref))):
        copies.append(pltpu.make_async_copy(source, to, in_sem.at[k]))
        copies[-1].start()
    chunks = net_hbm.shape[1] // LANES
    patch_pad = net_ref.shape[0] // (2 * chunks)
    loads = []
    for c in range(chunks):
        loads.append(pltpu.make_async_copy(
            net_hbm.at[:, pl.ds(c * LANES, LANES)], net_ref.at[pl.ds(c * patch_pad, patch_dev), :], net_sem.at[c]))
    for load in loads[:chunks // 2]:
        load.start()
    slot_ref[...] = jnp.zeros_like(slot_ref)
    blocks = patch_ref.shape[0]
    copies[0].wait()
    patch = patch_ref[...]
    owner = jnp.zeros_like(patch)
    for o in range(1, owners):
        owner += (patch >= o * patch_dev).astype(jnp.int32)
    local = patch - owner * patch_dev
    owner = owner ^ me

    lane = iota((LANES, LANES), 1)
    sub = iota((LANES, LANES), 0)
    upto = (sub <= lane).astype(jnp.bfloat16)
    every = jnp.ones((LANES, LANES), jnp.bfloat16)
    counter = jnp.concatenate([upto, every], axis=1)
    earlier = (iota((blocks, blocks), 1) < iota((blocks, blocks), 0)).astype(jnp.bfloat16)
    blane = iota((blocks, LANES), 1)
    diagonal = iota((blocks, blocks), 0) == iota((blocks, blocks), 1)

    key = jnp.zeros_like(patch)
    found = []
    for x in range(owners):
        mine = owner == x
        counts = jnp.dot(mine.astype(jnp.bfloat16), counter, preferred_element_type=jnp.float32)
        total = counts[:, LANES:]
        offset = jnp.dot(earlier, total.astype(jnp.bfloat16), preferred_element_type=jnp.float32)
        first = jnp.sum(jnp.where(diagonal, offset, 0.0), axis=0, keepdims=True)
        first = first.astype(jnp.int32) >> 7
        first_ref[x:x + 1, :] = first
        base_ref[x:x + 1, :] = (first + x * (windows + 1)) * 8
        before = counts[:, :LANES].astype(jnp.int32) - mine.astype(jnp.int32)
        edge = offset.astype(jnp.int32) & (LANES - 1)
        key = jnp.where(mine, before + edge + 2 * LANES * x, key)
        found.append((mine, before, edge, total.astype(jnp.int32)))
    copy = pltpu.make_async_copy(base_ref, base_smem, base_sem)
    copy.start()
    for load in loads[chunks // 2:]:
        load.start()
    for x in range(owners):
        mine, before, edge, total = found[x]
        word = jnp.where(mine, blane + LANES * (blane - before), 0)
        for bit in range(7):
            moves = 1 << (7 + bit)
            coming = pltpu.roll(word, LANES - (1 << bit), 1)
            word = jnp.where((coming & moves) != 0, coming, jnp.where((word & moves) != 0, 0, word))
        rank = (blane - edge) & (LANES - 1)
        source = take_lanes(word & (LANES - 1), rank)
        valid = rank < total
        code_ref[x * blocks:(x + 1) * blocks, :] = source + jnp.where(valid, jnp.where(blane >= edge, LANES, -LANES), 0)

    key_ref[...] = key
    for waiting in copies[1:]:
        waiting.wait()
    span = span_ref[...]
    row = (2 * ((span >> 1) * patch_pad + local) + (span & 1) + 1).astype(jnp.float32)
    for b in range(blocks):
        load_ref[8 * b:8 * b + 3, :] = target_ref[:, b * LANES:(b + 1) * LANES]
        load_ref[8 * b + 3:8 * b + 5, :] = (grid_ref[:, b * LANES:(b + 1) * LANES].astype(jnp.float32) + 0.5) * (1.0 / LEVELS)
        load_ref[8 * b + 5:8 * b + 6, :] = row[b:b + 1, :]
    copy.wait()

    def place(step, carry):
        for k in range(UNROLL):
            b = step * UNROLL + k
            load = load_ref[pl.ds(pl.multiple_of(8 * b, 8), 8), :]
            for o in range(owners):
                code = jnp.broadcast_to(code_ref[pl.ds(o * blocks + b, 1), :], (8, LANES))
                moved = take_lanes(load, code & (LANES - 1))
                base = pl.multiple_of(base_smem[o, b], 8)
                pltpu.store(slot_ref.at[pl.ds(base, 8), :], moved, mask=code >= LANES)
                pltpu.store(slot_ref.at[pl.ds(base + 8, 8), :], moved, mask=code < 0)
        return carry

    lax.fori_loop(0, blocks // UNROLL, place, 0)

    for x in range(owners):
        for c in range(SENT):
            for w in range(0, windows, 8):
                size = min(8, windows - w)
                rows = slot_ref[pl.ds((x * (windows + 1) + w) * 8 + c, size, stride=8), :]
                at = ((x % 2) * SENT + c) * windows + w
                sent_refs[x // 2][at:at + size, :] = rows
    for waiting in loads:
        waiting.wait()


def route(node_patch, node_span, start_grid, target, net, owners, windows):
    nodes = node_patch.shape[0]
    blocks = nodes // LANES
    patch_dev = net.shape[0]
    chunks = net.shape[1] // LANES
    patch_pad = round_up(patch_dev, 8)
    return pl.pallas_call(
        functools.partial(route_kernel, owners, windows, patch_dev),
        out_shape=(
            *[jax.ShapeDtypeStruct((2 * SENT * windows, LANES), jnp.float32)] * (owners // 2),
            jax.ShapeDtypeStruct((blocks, LANES), jnp.int32),
            jax.ShapeDtypeStruct((owners, blocks), jnp.int32),
            jax.ShapeDtypeStruct((2 * chunks * patch_pad, LANES), jnp.float32),
        ),
        in_specs=[pl.BlockSpec(memory_space=pltpu.HBM)] * 5,
        out_specs=[pl.BlockSpec(memory_space=pltpu.VMEM)] * (owners // 2 + 3),
        scratch_shapes=[
            pltpu.VMEM((blocks, LANES), jnp.int32),
            pltpu.VMEM((blocks, LANES), jnp.int32),
            pltpu.VMEM(start_grid.shape, jnp.int32),
            pltpu.VMEM(target.shape, jnp.float32),
            pltpu.VMEM((owners * blocks, LANES), jnp.int32),
            pltpu.VMEM((8 * blocks, LANES), jnp.float32),
            pltpu.VMEM((owners * (windows + 1) * 8, LANES), jnp.float32),
            pltpu.VMEM((owners, blocks), jnp.int32),
            pltpu.SMEM((owners, blocks), jnp.int32),
            pltpu.SemaphoreType.DMA((4,)),
            pltpu.SemaphoreType.DMA((chunks,)),
            pltpu.SemaphoreType.DMA,
        ],
        compiler_params=pltpu.CompilerParams(vmem_limit_bytes=16 * 2**20),
        name="route",
    )(*(pltpu.with_memory_space_constraint(x, pltpu.HBM) for x in (
        node_patch.reshape(blocks, LANES), node_span.reshape(blocks, LANES), start_grid, target, net)))


def bernstein(param):
    other = 1.0 - param
    square, cross, low = other * other, param * other, param * param
    value = (other * square, 3.0 * cross * other, 3.0 * param * cross, param * low)
    slope = (-3.0 * square, 3.0 * square - 6.0 * cross, 6.0 * cross - 3.0 * low, 3.0 * low)
    return value, slope


def weighted(weights, values):
    return (weights[0] * values[0] + weights[1] * values[1]) + (weights[2] * values[2] + weights[3] * values[3])


def surface(read, upar, vpar, answer):
    base_u, slope_u = bernstein(upar)
    base_v, slope_v = bernstein(vpar)
    yield
    point, along_u, along_v = [], [], []
    for c in range(4):
        mixed, mixed_u = [], []
        for j in range(4):
            column = [read(c * 16 + i * 4 + j) for i in range(4)]
            mixed.append(weighted(base_u, column))
            mixed_u.append(weighted(slope_u, column))
            yield
        point.append(weighted(base_v, mixed))
        along_u.append(weighted(base_v, mixed_u))
        along_v.append(weighted(slope_v, mixed))
        yield
    inverse = 1.0 / point[3]
    position = [point[c] * inverse for c in range(3)]
    yield
    tangent_u = [(along_u[c] - position[c] * along_u[3]) * inverse for c in range(3)]
    tangent_v = [(along_v[c] - position[c] * along_v[3]) * inverse for c in range(3)]
    yield
    answer.extend((position, tangent_u, tangent_v))


def inner(left, right):
    return left[0] * right[0] + left[1] * right[1] + left[2] * right[2]


def project(read, goal, start, finish):
    upar, vpar = start()
    goal = goal()
    for _ in range(ITERS):
        answer = []
        yield from surface(read, upar, vpar, answer)
        position, tangent_u, tangent_v = answer
        miss = [position[c] - goal[c] for c in range(3)]
        grad_u = inner(tangent_u, miss)
        grad_v = inner(tangent_v, miss)
        yield
        h_uu = inner(tangent_u, tangent_u) + damping
        h_vv = inner(tangent_v, tangent_v) + damping
        h_uv = inner(tangent_u, tangent_v)
        yield
        inverse = 1.0 / (h_uu * h_vv - h_uv * h_uv)
        upar = jnp.clip(upar - (h_vv * grad_u - h_uv * grad_v) * inverse, 0.0, 1.0)
        vpar = jnp.clip(vpar - (h_uu * grad_v - h_uv * grad_u) * inverse, 0.0, 1.0)
        yield
    answer = []
    yield from surface(read, upar, vpar, answer)
    finish(answer[0] + answer[1] + answer[2])


PROJECT_STEPS = ITERS * 27 + 25


def project_kernel(pairs, windows, given_pad, *refs):
    got_refs, (_, other_ref), out_refs = refs[:pairs], refs[pairs:pairs + 2], refs[pairs + 2:2 * pairs + 2]
    (net_ref, load_ref, index_ref, index_0, index_1, index_2, index_3,
     tile_even, tile_odd, turn_even, turn_odd, coeff_ref, index_sem, net_sem) = refs[2 * pairs + 2:]
    per = 8 // pairs
    half = windows // per
    total = 2 * half
    rows = net_ref.shape[0] // 2
    indices = (index_0, index_1, index_2, index_3)
    tiles, turns = (tile_even, tile_odd), (turn_even, turn_odd)
    depth = len(indices)
    patches, chunks = other_ref.shape[0], other_ref.shape[1] // LANES
    patch_pad = rows // chunks

    def arrived(t, c):
        return load_ref[pl.ds(pl.multiple_of((t * SENT + c) * 8, 8), 8), :]

    def fetch(t, k):
        return pltpu.make_async_copy(
            index_ref.at[pl.ds(pl.multiple_of(8 * t, 8), 8), :], indices[k % depth], index_sem.at[k % depth])

    def partner(c):
        return pltpu.make_async_copy(
            other_ref.at[:, pl.ds(c * LANES, LANES)], net_ref.at[pl.ds(rows + c * patch_pad, patches), :], net_sem.at[c])

    def gather(k):
        index, tile = indices[k % depth], tiles[k % 2]
        for s in range(8):
            for i in range(LANES):
                tile[s * LANES + i:s * LANES + i + 1, :] = net_ref[pl.ds(index[s, i], 1), :]
                yield

    def turn(k):
        tile, turned = tiles[k % 2], turns[k % 2]
        for s in range(8):
            turned[pl.ds(s, LANES, stride=8), :] = tile[s * LANES:(s + 1) * LANES, :].T
            yield

    def solve(t, k):
        turned = turns[k % 2]
        odd = (arrived(t, SENT - 1).astype(jnp.int32) & 1) == 0
        kept = set()

        def read(e):
            at = slice(8 * e, 8 * e + 8)
            if e not in kept:
                kept.add(e)
                coeff_ref[at, :] = jnp.where(odd, turned[512 + 8 * e:520 + 8 * e, :], turned[at, :])
            return coeff_ref[at, :]

        def finish(result):
            base = t // half * given_pad + t % half * per
            for c in range(GIVEN):
                at = (c + 1) % GIVEN
                for j in range(pairs):
                    out_refs[j][pl.ds(base + at * windows, per), :] = result[c][j * per:(j + 1) * per, :]

        return project(
            read,
            lambda: [arrived(t, c) for c in range(3)],
            lambda: (arrived(t, 3), arrived(t, 4)),
            finish)

    def interleave(*works):
        order = sorted(((at + 0.5) / size, k) for k, (_, size) in enumerate(works) for at in range(size))
        for _, k in order:
            next(works[k][0], None)
        for work, _ in works:
            for _ in work:
                pass

    def gathering(k):
        return gather(k), 8 * LANES

    def turning(k):
        return turn(k), 8

    def solving(t, k):
        return solve(t, k), PROJECT_STEPS

    def collect(t, c):
        at = (t // half * SENT + c) * windows + t % half * per
        for j in range(pairs):
            to = (t * SENT + c) * 8 + j * per
            load_ref[to:to + per, :] = got_refs[j][at:at + per, :]

    for t in range(total):
        collect(t, SENT - 1)
        index_ref[8 * t:8 * t + 8, :] = (jnp.maximum(arrived(t, SENT - 1).astype(jnp.int32) - 1, 0) >> 1) + t // half * rows
        if t < depth:
            fetch(t, t).start()
    for c in range(chunks):
        partner(c).start()
    for t in range(total):
        for c in range(SENT - 1):
            collect(t, c)
    index_ref[8 * total:8 * total + 16, :] = jnp.zeros((16, LANES), jnp.int32)
    fetch(0, 0).wait()
    interleave(gathering(0))
    fetch(depth, depth).start()
    fetch(1, 1).wait()
    interleave(gathering(1), turning(0))
    fetch(depth + 1, depth + 1).start()

    def steps(i, carry):
        @pl.when(i == -(-(half - depth - 1) // depth))
        def _():
            for c in range(chunks):
                partner(c).wait()

        for k in range(depth):
            t = depth * i + k
            fetch(t + 2, k + 2).wait()
            interleave(gathering(k + 2), turning(k + 1), solving(t, k))
            fetch(t + depth + 2, k + 2).start()
        return carry

    lax.fori_loop(0, total // depth - 1, steps, 0)
    used = jnp.max(jnp.maximum(arrived(total - 2, SENT - 1), arrived(total - 1, SENT - 1))) > 0.0

    @pl.when(used)
    def _():
        for t in range(total - depth, total):
            if t + 2 < total:
                fetch(t + 2, t + 2).wait()
                interleave(gathering(t + 2), turning(t + 1), solving(t, t))
            elif t + 1 < total:
                interleave(turning(t + 1), solving(t, t))
            else:
                interleave(solving(t, t))

    @pl.when(jnp.logical_not(used))
    def _():
        for t in (total - 2, total - 1):
            fetch(t, t).wait()
        interleave(turning(total - 3), solving(total - 4, total - 4))
        interleave(solving(total - 3, total - 3))

    for t in (total, total + 1):
        fetch(t, t).wait()


def project_nodes(got, net_rows, other, windows, given_pad):
    pairs = len(got)
    chunks = other.shape[1] // LANES
    tiles = 2 * pairs * windows
    return pl.pallas_call(
        functools.partial(project_kernel, pairs, windows, given_pad),
        out_shape=(
            *[jax.ShapeDtypeStruct((2 * given_pad, LANES), jnp.float32)] * pairs,
            jax.ShapeDtypeStruct(net_rows.shape, jnp.float32),
        ),
        in_specs=[pl.BlockSpec(memory_space=pltpu.VMEM)] * (pairs + 1) + [pl.BlockSpec(memory_space=pl.ANY)],
        out_specs=[pl.BlockSpec(memory_space=pltpu.VMEM)] * (pairs + 1),
        input_output_aliases={pairs: pairs},
        scratch_shapes=[
            pltpu.VMEM((tiles * SENT, LANES), jnp.float32),
            pltpu.VMEM((tiles + 16, LANES), jnp.int32),
            pltpu.SMEM((8, LANES), jnp.int32),
            pltpu.SMEM((8, LANES), jnp.int32),
            pltpu.SMEM((8, LANES), jnp.int32),
            pltpu.SMEM((8, LANES), jnp.int32),
            pltpu.VMEM((8 * LANES, LANES), jnp.float32),
            pltpu.VMEM((8 * LANES, LANES), jnp.float32),
            pltpu.VMEM((8 * LANES, LANES), jnp.float32),
            pltpu.VMEM((8 * LANES, LANES), jnp.float32),
            pltpu.VMEM((64 * 8, LANES), jnp.float32),
            pltpu.SemaphoreType.DMA((4,)),
            pltpu.SemaphoreType.DMA((chunks,)),
        ],
        compiler_params=pltpu.CompilerParams(vmem_limit_bytes=12 * 2**20),
        name="project",
    )(*got, net_rows, other)[:pairs]


def return_kernel(owners, windows, given_pad, key_ref, first_smem, *refs):
    got_refs, (out_hbm, out_ref, out_sem) = refs[:-3], refs[-3:]
    blocks = key_ref.shape[0]
    sub = iota((8, LANES), 0)

    def fetch(step, carry):
        for k in range(UNROLL):
            b = step * UNROLL + k
            key = jnp.broadcast_to(key_ref[pl.ds(b, 1), :], (8, LANES))
            lane = key & (LANES - 1)
            key = key >> 7
            rest = jnp.where(sub < 2, key - sub, -1)
            main = jnp.zeros((8, LANES), jnp.float32)
            last = jnp.zeros((8, LANES), jnp.float32)
            for x in range(owners):
                got_ref = got_refs[x // 2]
                base = (x % 2) * given_pad + first_smem[x, b]
                moved = take_lanes(got_ref[pl.ds(base, 8), :], lane)
                last = jnp.where(rest == 2 * x, moved, last)
                for step_over in range(2):
                    rows = got_ref[pl.ds(base + windows + step_over, 8, stride=windows), :]
                    main = jnp.where(key == 2 * x + step_over, take_lanes(rows, lane), main)
            at = pl.ds(pl.multiple_of(b * LANES, LANES), LANES)
            out_ref[0:8, at] = main
            out_ref[8:9, at] = jnp.sum(last, axis=0, keepdims=True)
        return carry

    trips = blocks // UNROLL
    parts = 4 if trips % 4 == 0 else 1
    copies = []
    for part in range(parts):
        lax.fori_loop(part * trips // parts, (part + 1) * trips // parts, fetch, 0)
        at = pl.ds(part * blocks // parts * LANES, blocks // parts * LANES)
        copies.append(pltpu.make_async_copy(out_ref.at[:, at], out_hbm.at[:, at], out_sem.at[part]))
        copies[-1].start()
    for copy in copies:
        copy.wait()


def return_nodes(key, first, got, windows, given_pad):
    owners, blocks = first.shape
    return pl.pallas_call(
        functools.partial(return_kernel, owners, windows, given_pad),
        out_shape=jax.ShapeDtypeStruct((GIVEN, blocks * LANES), jnp.float32),
        in_specs=[
            pl.BlockSpec(memory_space=pltpu.VMEM),
            pl.BlockSpec(memory_space=pltpu.SMEM),
        ] + [pl.BlockSpec(memory_space=pltpu.VMEM)] * len(got),
        out_specs=pl.BlockSpec(memory_space=pltpu.HBM),
        scratch_shapes=[pltpu.VMEM((GIVEN, blocks * LANES), jnp.float32), pltpu.SemaphoreType.DMA((4,))],
        compiler_params=pltpu.CompilerParams(vmem_limit_bytes=16 * 2**20),
        name="give_back",
    )(key, first, *got)


def body(node_patch, node_span, start_grid, target, net):
    owners = lax.axis_size("bulk")
    windows = node_patch.shape[0] * 5 // 32 // LANES
    given_pad = round_up(GIVEN * windows + 1, 8)
    def swap(value, distance):
        return lax.ppermute(value, "bulk", [(i, i ^ distance) for i in range(owners)])

    def swap_pairs(values):
        return [swap(value, 2 * j) if j else value for j, value in enumerate(values)]

    other = swap(net, 1)
    *sent, key, first, net_rows = route(node_patch, node_span, start_grid, target, net, owners, windows)
    placed = project_nodes(swap_pairs(sent), net_rows, other, windows, given_pad)
    return return_nodes(key, first, swap_pairs(placed), windows, given_pad)


def solution(mesh):
    return jax.shard_map(
        body,
        mesh=mesh,
        in_specs=(
            P(("dom", "bulk")),
            P(("dom", "bulk")),
            P(None, ("dom", "bulk")),
            P(None, ("dom", "bulk")),
            P("bulk", None),
        ),
        out_specs=P(None, ("dom", "bulk")),
        check_vma=False,
    )
```

```python
import functools

import jax
import jax.numpy as jnp
from jax import lax
from jax.experimental import pallas as pl
from jax.experimental.pallas import tpu as pltpu
from jax.sharding import PartitionSpec as P

SPANS = 16
LEVELS = 16
ITERS = 4
LANES = 128
SENT = 6
GIVEN = 9
UNROLL = 32

damping = 0.1


def round_up(value, unit):
    return -(-value // unit) * unit


def iota(shape, dim):
    return lax.broadcasted_iota(jnp.int32, shape, dim)


def take_lanes(rows, lane):
    return jnp.take_along_axis(rows, lane, axis=1, mode="promise_in_bounds")


def route_kernel(owners, windows, patch_dev, patch_hbm, span_hbm, grid_hbm, target_hbm, net_hbm,
                 *refs):
    sent_refs = refs[:owners // 2]
    (key_ref, first_ref, net_ref, patch_ref, span_ref, grid_ref, target_ref,
     code_ref, load_ref, slot_ref, base_ref, base_smem, in_sem, net_sem, base_sem) = refs[owners // 2:]
    me = lax.axis_index("bulk")
    copies = []
    for k, (source, to) in enumerate(
            ((patch_hbm, patch_ref), (span_hbm, span_ref), (grid_hbm, grid_ref), (target_hbm, target_ref))):
        copies.append(pltpu.make_async_copy(source, to, in_sem.at[k]))
        copies[-1].start()
    chunks = net_hbm.shape[1] // LANES
    patch_pad = net_ref.shape[0] // (2 * chunks)
    loads = []
    for c in range(chunks):
        loads.append(pltpu.make_async_copy(
            net_hbm.at[:, pl.ds(c * LANES, LANES)], net_ref.at[pl.ds(c * patch_pad, patch_dev), :], net_sem.at[c]))
    for load in loads[:chunks // 2]:
        load.start()
    slot_ref[...] = jnp.zeros_like(slot_ref)
    blocks = patch_ref.shape[0]
    copies[0].wait()
    patch = patch_ref[...]
    owner = jnp.zeros_like(patch)
    for o in range(1, owners):
        owner += (patch >= o * patch_dev).astype(jnp.int32)
    local = patch - owner * patch_dev
    owner = owner ^ me

    lane = iota((LANES, LANES), 1)
    sub = iota((LANES, LANES), 0)
    upto = (sub <= lane).astype(jnp.bfloat16)
    every = jnp.ones((LANES, LANES), jnp.bfloat16)
    counter = jnp.concatenate([upto, every], axis=1)
    earlier = (iota((blocks, blocks), 1) < iota((blocks, blocks), 0)).astype(jnp.bfloat16)
    blane = iota((blocks, LANES), 1)
    diagonal = iota((blocks, blocks), 0) == iota((blocks, blocks), 1)

    key = jnp.zeros_like(patch)
    found = []
    for x in range(owners):
        mine = owner == x
        counts = jnp.dot(mine.astype(jnp.bfloat16), counter, preferred_element_type=jnp.float32)
        total = counts[:, LANES:]
        offset = jnp.dot(earlier, total.astype(jnp.bfloat16), preferred_element_type=jnp.float32)
        first = jnp.sum(jnp.where(diagonal, offset, 0.0), axis=0, keepdims=True)
        first = first.astype(jnp.int32) >> 7
        first_ref[x:x + 1, :] = first
        base_ref[x:x + 1, :] = (first + x * (windows + 1)) * 8
        before = counts[:, :LANES].astype(jnp.int32) - mine.astype(jnp.int32)
        edge = offset.astype(jnp.int32) & (LANES - 1)
        key = jnp.where(mine, before + edge + 2 * LANES * x, key)
        found.append((mine, before, edge, total.astype(jnp.int32)))
    copy = pltpu.make_async_copy(base_ref, base_smem, base_sem)
    copy.start()
    for load in loads[chunks // 2:]:
        load.start()
    for x in range(owners):
        mine, before, edge, total = found[x]
        word = jnp.where(mine, blane + LANES * (blane - before), 0)
        for bit in range(7):
            moves = 1 << (7 + bit)
            coming = pltpu.roll(word, LANES - (1 << bit), 1)
            word = jnp.where((coming & moves) != 0, coming, jnp.where((word & moves) != 0, 0, word))
        rank = (blane - edge) & (LANES - 1)
        source = take_lanes(word & (LANES - 1), rank)
        valid = rank < total
        code_ref[x * blocks:(x + 1) * blocks, :] = source + jnp.where(valid, jnp.where(blane >= edge, LANES, -LANES), 0)

    key_ref[...] = key
    for waiting in copies[1:]:
        waiting.wait()
    span = span_ref[...]
    row = (2 * ((span >> 1) * patch_pad + local) + (span & 1) + 1).astype(jnp.float32)
    for b in range(blocks):
        load_ref[8 * b:8 * b + 3, :] = target_ref[:, b * LANES:(b + 1) * LANES]
        load_ref[8 * b + 3:8 * b + 5, :] = (grid_ref[:, b * LANES:(b + 1) * LANES].astype(jnp.float32) + 0.5) * (1.0 / LEVELS)
        load_ref[8 * b + 5:8 * b + 6, :] = row[b:b + 1, :]
    copy.wait()

    def place(step, carry):
        for k in range(UNROLL):
            b = step * UNROLL + k
            load = load_ref[pl.ds(pl.multiple_of(8 * b, 8), 8), :]
            for o in range(owners):
                code = jnp.broadcast_to(code_ref[pl.ds(o * blocks + b, 1), :], (8, LANES))
                moved = take_lanes(load, code & (LANES - 1))
                base = pl.multiple_of(base_smem[o, b], 8)
                pltpu.store(slot_ref.at[pl.ds(base, 8), :], moved, mask=code >= LANES)
                pltpu.store(slot_ref.at[pl.ds(base + 8, 8), :], moved, mask=code < 0)
        return carry

    lax.fori_loop(0, blocks // UNROLL, place, 0)

    for x in range(owners):
        for c in range(SENT):
            for w in range(0, windows, 8):
                size = min(8, windows - w)
                rows = slot_ref[pl.ds((x * (windows + 1) + w) * 8 + c, size, stride=8), :]
                at = ((x % 2) * SENT + c) * windows + w
                sent_refs[x // 2][at:at + size, :] = rows
    for waiting in loads:
        waiting.wait()


def route(node_patch, node_span, start_grid, target, net, owners, windows):
    nodes = node_patch.shape[0]
    blocks = nodes // LANES
    patch_dev = net.shape[0]
    chunks = net.shape[1] // LANES
    patch_pad = round_up(patch_dev, 8)
    return pl.pallas_call(
        functools.partial(route_kernel, owners, windows, patch_dev),
        out_shape=(
            *[jax.ShapeDtypeStruct((2 * SENT * windows, LANES), jnp.float32)] * (owners // 2),
            jax.ShapeDtypeStruct((blocks, LANES), jnp.int32),
            jax.ShapeDtypeStruct((owners, blocks), jnp.int32),
            jax.ShapeDtypeStruct((2 * chunks * patch_pad, LANES), jnp.float32),
        ),
        in_specs=[pl.BlockSpec(memory_space=pltpu.HBM)] * 5,
        out_specs=[pl.BlockSpec(memory_space=pltpu.VMEM)] * (owners // 2 + 3),
        scratch_shapes=[
            pltpu.VMEM((blocks, LANES), jnp.int32),
            pltpu.VMEM((blocks, LANES), jnp.int32),
            pltpu.VMEM(start_grid.shape, jnp.int32),
            pltpu.VMEM(target.shape, jnp.float32),
            pltpu.VMEM((owners * blocks, LANES), jnp.int32),
            pltpu.VMEM((8 * blocks, LANES), jnp.float32),
            pltpu.VMEM((owners * (windows + 1) * 8, LANES), jnp.float32),
            pltpu.VMEM((owners, blocks), jnp.int32),
            pltpu.SMEM((owners, blocks), jnp.int32),
            pltpu.SemaphoreType.DMA((4,)),
            pltpu.SemaphoreType.DMA((chunks,)),
            pltpu.SemaphoreType.DMA,
        ],
        compiler_params=pltpu.CompilerParams(vmem_limit_bytes=16 * 2**20),
        name="route",
    )(*(pltpu.with_memory_space_constraint(x, pltpu.HBM) for x in (
        node_patch.reshape(blocks, LANES), node_span.reshape(blocks, LANES), start_grid, target, net)))


def bernstein(param):
    other = 1.0 - param
    square, cross, low = other * other, param * other, param * param
    value = (other * square, 3.0 * cross * other, 3.0 * param * cross, param * low)
    slope = (-3.0 * square, 3.0 * square - 6.0 * cross, 6.0 * cross - 3.0 * low, 3.0 * low)
    return value, slope


def weighted(weights, values):
    return (weights[0] * values[0] + weights[1] * values[1]) + (weights[2] * values[2] + weights[3] * values[3])


def surface(read, upar, vpar, answer):
    base_u, slope_u = bernstein(upar)
    base_v, slope_v = bernstein(vpar)
    yield
    point, along_u, along_v = [], [], []
    for c in range(4):
        mixed, mixed_u = [], []
        for j in range(4):
            column = [read(c * 16 + i * 4 + j) for i in range(4)]
            mixed.append(weighted(base_u, column))
            mixed_u.append(weighted(slope_u, column))
            yield
        point.append(weighted(base_v, mixed))
        along_u.append(weighted(base_v, mixed_u))
        along_v.append(weighted(slope_v, mixed))
        yield
    inverse = 1.0 / point[3]
    position = [point[c] * inverse for c in range(3)]
    yield
    tangent_u = [(along_u[c] - position[c] * along_u[3]) * inverse for c in range(3)]
    tangent_v = [(along_v[c] - position[c] * along_v[3]) * inverse for c in range(3)]
    yield
    answer.extend((position, tangent_u, tangent_v))


def inner(left, right):
    return left[0] * right[0] + left[1] * right[1] + left[2] * right[2]


def project(read, goal, start, finish):
    upar, vpar = start()
    goal = goal()
    for _ in range(ITERS):
        answer = []
        yield from surface(read, upar, vpar, answer)
        position, tangent_u, tangent_v = answer
        miss = [position[c] - goal[c] for c in range(3)]
        grad_u = inner(tangent_u, miss)
        grad_v = inner(tangent_v, miss)
        yield
        h_uu = inner(tangent_u, tangent_u) + damping
        h_vv = inner(tangent_v, tangent_v) + damping
        h_uv = inner(tangent_u, tangent_v)
        yield
        inverse = 1.0 / (h_uu * h_vv - h_uv * h_uv)
        upar = jnp.clip(upar - (h_vv * grad_u - h_uv * grad_v) * inverse, 0.0, 1.0)
        vpar = jnp.clip(vpar - (h_uu * grad_v - h_uv * grad_u) * inverse, 0.0, 1.0)
        yield
    answer = []
    yield from surface(read, upar, vpar, answer)
    finish(answer[0] + answer[1] + answer[2])


PROJECT_STEPS = ITERS * 27 + 25


def project_kernel(pairs, windows, given_pad, *refs):
    got_refs, (_, other_ref), out_refs = refs[:pairs], refs[pairs:pairs + 2], refs[pairs + 2:2 * pairs + 2]
    (net_ref, load_ref, index_ref, index_0, index_1, index_2, index_3,
     tile_even, tile_odd, turn_even, turn_odd, coeff_ref, index_sem, net_sem) = refs[2 * pairs + 2:]
    per = 8 // pairs
    half = windows // per
    total = 2 * half
    rows = net_ref.shape[0] // 2
    indices = (index_0, index_1, index_2, index_3)
    tiles, turns = (tile_even, tile_odd), (turn_even, turn_odd)
    depth = len(indices)
    patches, chunks = other_ref.shape[0], other_ref.shape[1] // LANES
    patch_pad = rows // chunks

    def arrived(t, c):
        return load_ref[pl.ds(pl.multiple_of((t * SENT + c) * 8, 8), 8), :]

    def fetch(t, k):
        return pltpu.make_async_copy(
            index_ref.at[pl.ds(pl.multiple_of(8 * t, 8), 8), :], indices[k % depth], index_sem.at[k % depth])

    def partner(c):
        return pltpu.make_async_copy(
            other_ref.at[:, pl.ds(c * LANES, LANES)], net_ref.at[pl.ds(rows + c * patch_pad, patches), :], net_sem.at[c])

    def gather(k):
        index, tile = indices[k % depth], tiles[k % 2]
        for s in range(8):
            for i in range(LANES):
                tile[s * LANES + i:s * LANES + i + 1, :] = net_ref[pl.ds(index[s, i], 1), :]
                yield

    def turn(k):
        tile, turned = tiles[k % 2], turns[k % 2]
        for s in range(8):
            turned[pl.ds(s, LANES, stride=8), :] = tile[s * LANES:(s + 1) * LANES, :].T
            yield

    def solve(t, k):
        turned = turns[k % 2]
        odd = (arrived(t, SENT - 1).astype(jnp.int32) & 1) == 0
        kept = set()

        def read(e):
            at = slice(8 * e, 8 * e + 8)
            if e not in kept:
                kept.add(e)
                coeff_ref[at, :] = jnp.where(odd, turned[512 + 8 * e:520 + 8 * e, :], turned[at, :])
            return coeff_ref[at, :]

        def finish(result):
            base = owner_of(t) * given_pad + t % half * per
            for c in range(GIVEN):
                at = (c + 1) % GIVEN
                for j in range(pairs):
                    out_refs[j][pl.ds(base + at * windows, per), :] = result[c][j * per:(j + 1) * per, :]

        return project(
            read,
            lambda: [arrived(t, c) for c in range(3)],
            lambda: (arrived(t, 3), arrived(t, 4)),
            finish)

    def interleave(*works):
        order = sorted(((at + 0.5) / size, k) for k, (_, size) in enumerate(works) for at in range(size))
        for _, k in order:
            next(works[k][0], None)
        for work, _ in works:
            for _ in work:
                pass

    def gathering(k):
        return gather(k), 8 * LANES

    def turning(k):
        return turn(k), 8

    def solving(t, k):
        return solve(t, k), PROJECT_STEPS

    at = SENT * windows - 2 * per
    tail = got_refs[0][at:at + 2 * per, :]
    for j in range(1, pairs):
        tail = jnp.maximum(tail, got_refs[j][at:at + 2 * per, :])
    turned_round = jnp.where(jnp.max(tail) > 0.0, 0, 1)

    def owner_of(t):
        return t // half ^ turned_round

    def collect(t, c):
        at = (owner_of(t) * SENT + c) * windows + t % half * per
        for j in range(pairs):
            to = (t * SENT + c) * 8 + j * per
            load_ref[to:to + per, :] = got_refs[j][pl.ds(at, per), :]

    for t in range(total):
        collect(t, SENT - 1)
        index_ref[8 * t:8 * t + 8, :] = (jnp.maximum(arrived(t, SENT - 1).astype(jnp.int32) - 1, 0) >> 1) + owner_of(t) * rows
        if t < depth:
            fetch(t, t).start()
    for c in range(chunks):
        partner(c).start()
    for t in range(total):
        for c in range(SENT - 1):
            collect(t, c)
    for c in range(chunks):
        partner(c).wait()
    index_ref[8 * total:8 * total + 16, :] = jnp.zeros((16, LANES), jnp.int32)
    fetch(0, 0).wait()
    interleave(gathering(0))
    fetch(depth, depth).start()
    fetch(1, 1).wait()
    interleave(gathering(1), turning(0))
    fetch(depth + 1, depth + 1).start()

    def steps(i, carry):
        for k in range(depth):
            t = depth * i + k
            fetch(t + 2, k + 2).wait()
            interleave(gathering(k + 2), turning(k + 1), solving(t, k))
            fetch(t + depth + 2, k + 2).start()
        return carry

    lax.fori_loop(0, total // depth - 1, steps, 0)
    used = jnp.max(jnp.maximum(arrived(total - 2, SENT - 1), arrived(total - 1, SENT - 1))) > 0.0

    @pl.when(used)
    def _():
        for t in range(total - depth, total):
            if t + 2 < total:
                fetch(t + 2, t + 2).wait()
                interleave(gathering(t + 2), turning(t + 1), solving(t, t))
            elif t + 1 < total:
                interleave(turning(t + 1), solving(t, t))
            else:
                interleave(solving(t, t))

    @pl.when(jnp.logical_not(used))
    def _():
        for t in (total - 2, total - 1):
            fetch(t, t).wait()
        interleave(turning(total - 3), solving(total - 4, total - 4))
        interleave(solving(total - 3, total - 3))

    for t in (total, total + 1):
        fetch(t, t).wait()


def project_nodes(got, net_rows, other, windows, given_pad):
    pairs = len(got)
    chunks = other.shape[1] // LANES
    tiles = 2 * pairs * windows
    return pl.pallas_call(
        functools.partial(project_kernel, pairs, windows, given_pad),
        out_shape=(
            *[jax.ShapeDtypeStruct((2 * given_pad, LANES), jnp.float32)] * pairs,
            jax.ShapeDtypeStruct(net_rows.shape, jnp.float32),
        ),
        in_specs=[pl.BlockSpec(memory_space=pltpu.VMEM)] * (pairs + 1) + [pl.BlockSpec(memory_space=pl.ANY)],
        out_specs=[pl.BlockSpec(memory_space=pltpu.VMEM)] * (pairs + 1),
        input_output_aliases={pairs: pairs},
        scratch_shapes=[
            pltpu.VMEM((tiles * SENT, LANES), jnp.float32),
            pltpu.VMEM((tiles + 16, LANES), jnp.int32),
            pltpu.SMEM((8, LANES), jnp.int32),
            pltpu.SMEM((8, LANES), jnp.int32),
            pltpu.SMEM((8, LANES), jnp.int32),
            pltpu.SMEM((8, LANES), jnp.int32),
            pltpu.VMEM((8 * LANES, LANES), jnp.float32),
            pltpu.VMEM((8 * LANES, LANES), jnp.float32),
            pltpu.VMEM((8 * LANES, LANES), jnp.float32),
            pltpu.VMEM((8 * LANES, LANES), jnp.float32),
            pltpu.VMEM((64 * 8, LANES), jnp.float32),
            pltpu.SemaphoreType.DMA((4,)),
            pltpu.SemaphoreType.DMA((chunks,)),
        ],
        compiler_params=pltpu.CompilerParams(vmem_limit_bytes=12 * 2**20),
        name="project",
    )(*got, net_rows, other)[:pairs]


def return_kernel(owners, windows, given_pad, key_ref, first_smem, *refs):
    got_refs, (out_hbm, out_ref, out_sem) = refs[:-3], refs[-3:]
    blocks = key_ref.shape[0]
    sub = iota((8, LANES), 0)

    def fetch(step, carry):
        for k in range(UNROLL):
            b = step * UNROLL + k
            key = jnp.broadcast_to(key_ref[pl.ds(b, 1), :], (8, LANES))
            lane = key & (LANES - 1)
            key = key >> 7
            rest = jnp.where(sub < 2, key - sub, -1)
            main = jnp.zeros((8, LANES), jnp.float32)
            last = jnp.zeros((8, LANES), jnp.float32)
            for x in range(owners):
                got_ref = got_refs[x // 2]
                base = (x % 2) * given_pad + first_smem[x, b]
                moved = take_lanes(got_ref[pl.ds(base, 8), :], lane)
                last = jnp.where(rest == 2 * x, moved, last)
                for step_over in range(2):
                    rows = got_ref[pl.ds(base + windows + step_over, 8, stride=windows), :]
                    main = jnp.where(key == 2 * x + step_over, take_lanes(rows, lane), main)
            at = pl.ds(pl.multiple_of(b * LANES, LANES), LANES)
            out_ref[0:8, at] = main
            out_ref[8:9, at] = jnp.sum(last, axis=0, keepdims=True)
        return carry

    trips = blocks // UNROLL
    parts = 4 if trips % 4 == 0 else 1
    copies = []
    for part in range(parts):
        lax.fori_loop(part * trips // parts, (part + 1) * trips // parts, fetch, 0)
        at = pl.ds(part * blocks // parts * LANES, blocks // parts * LANES)
        copies.append(pltpu.make_async_copy(out_ref.at[:, at], out_hbm.at[:, at], out_sem.at[part]))
        copies[-1].start()
    for copy in copies:
        copy.wait()


def return_nodes(key, first, got, windows, given_pad):
    owners, blocks = first.shape
    return pl.pallas_call(
        functools.partial(return_kernel, owners, windows, given_pad),
        out_shape=jax.ShapeDtypeStruct((GIVEN, blocks * LANES), jnp.float32),
        in_specs=[
            pl.BlockSpec(memory_space=pltpu.VMEM),
            pl.BlockSpec(memory_space=pltpu.SMEM),
        ] + [pl.BlockSpec(memory_space=pltpu.VMEM)] * len(got),
        out_specs=pl.BlockSpec(memory_space=pltpu.HBM),
        scratch_shapes=[pltpu.VMEM((GIVEN, blocks * LANES), jnp.float32), pltpu.SemaphoreType.DMA((4,))],
        compiler_params=pltpu.CompilerParams(vmem_limit_bytes=16 * 2**20),
        name="give_back",
    )(key, first, *got)


def body(node_patch, node_span, start_grid, target, net):
    owners = lax.axis_size("bulk")
    windows = node_patch.shape[0] * 5 // 32 // LANES
    given_pad = round_up(GIVEN * windows + 1, 8)
    def swap(value, distance):
        return lax.ppermute(value, "bulk", [(i, i ^ distance) for i in range(owners)])

    def swap_pairs(values):
        return [swap(value, 2 * j) if j else value for j, value in enumerate(values)]

    other = swap(net, 1)
    *sent, key, first, net_rows = route(node_patch, node_span, start_grid, target, net, owners, windows)
    placed = project_nodes(swap_pairs(sent), net_rows, other, windows, given_pad)
    return return_nodes(key, first, swap_pairs(placed), windows, given_pad)


def solution(mesh):
    return jax.shard_map(
        body,
        mesh=mesh,
        in_specs=(
            P(("dom", "bulk")),
            P(("dom", "bulk")),
            P(None, ("dom", "bulk")),
            P(None, ("dom", "bulk")),
            P("bulk", None),
        ),
        out_specs=P(None, ("dom", "bulk")),
        check_vma=False,
    )
```
